32 devices in a mesh: ccd: 4 (over y, core), strip: 8 (over z, x).
Axes of the slice: x: 2, y: 2, z: 4, core: 2. Of those that a mesh axis runs over, the one named last changes fastest.
Arguments:
- tile_store: float32 [576, 16, 128], P(('ccd', 'strip')), may hold values from -13 to 13
- tile_source: int32 [32, 18], replicated, may hold values from 0 to 31, as said below
- tile_slot: int32 [32, 18], replicated, may hold values from 0 to 17, as said below
- shift_cols: int32 [4], P('ccd'), may hold values from -117 to 117
- spatial_order: int32 [4], P('ccd'), may hold values from 0 to 2
- science: float32 [512, 2048], P(('ccd', 'strip')), may hold values from -16 to 16
Outputs:
- difference: float32 [512, 2048], P(('ccd', 'strip'))
The draws below stay inside these ranges and needn't reach their ends.
Inputs may be any that keep to these rules, and one draw needn't show every extreme that they name: `tile_source`: every device holds exactly 18 tiles over all strips, one device holds at most 1 tiles of one strip, and some device holds exactly 1 tiles of some strip. `tile_slot`: each position of each store is named by exactly one pair of strip and tile.
All inputs are finite; a program needn't handle non-finite values.
Results may differ from the reference program's by a relative error of at most 0.005.
Values sent between devices are 32-bit elements; how exact they have to be, the bound alone decides.
No kernel may reach another device: no remote copies, remote signals or barrier semaphores. Data moves between devices by JAX's collectives and lax.ppermute only.
A program may use at most 64 MiB of HBM per device.

```python
import jax
import jax.numpy as jnp
from jax import lax

ROWS = 16
COLS = 2048
H = 11
CM = 128
TR = 16
TC = 128
RB = 4
NB = 27
NSP = 6
TW = 2304
TILES = 18
N_CCD = 4
N_STRIP = 8
DEVICES = 32


def gaussian_smooth(window, sigma_value, out_rows, out_cols):
    offsets = jnp.arange(-H, H + 1).astype(jnp.float32)
    weights = jnp.exp(-offsets * offsets / (2.0 * sigma_value * sigma_value))
    weights = weights / jnp.sum(weights)
    vertical = jnp.zeros((out_rows, window.shape[1]), jnp.float32)
    for tap_id in range(2 * H + 1):
        vertical = vertical + weights[tap_id] * window[tap_id:tap_id + out_rows, :]
    result = jnp.zeros((out_rows, out_cols), jnp.float32)
    for tap_id in range(2 * H + 1):
        result = result + weights[tap_id] * vertical[:, tap_id:tap_id + out_cols]
    return result


def shared_draw(key):
    key_perm = jax.random.fold_in(key, 11)
    key_devices = jax.random.fold_in(key, 12)
    key_order = jax.random.fold_in(key, 13)
    key_image = jax.random.fold_in(key, 14)
    key_shift = jax.random.fold_in(key, 15)
    key_noise = jax.random.fold_in(key, 16)
    per_dest = jax.vmap(lambda sub_key: jax.random.permutation(sub_key, TILES))(jax.random.split(key_perm, DEVICES))
    device_perm = jax.random.permutation(key_devices, DEVICES).astype(jnp.int32)
    residue = (per_dest.astype(jnp.int32) + jnp.arange(DEVICES, dtype=jnp.int32)[:, None]) % DEVICES
    owners = device_perm[residue].astype(jnp.int32)
    ranking = jax.random.permutation(key_order, DEVICES * TILES).astype(jnp.int32)
    composite = owners.reshape(-1) * (DEVICES * TILES) + ranking
    position = jnp.argsort(jnp.argsort(composite)).astype(jnp.int32)
    slots = (position - owners.reshape(-1) * TILES).reshape(DEVICES, TILES).astype(jnp.int32)
    images = 3.0 * jax.random.truncated_normal(key_image, -4.0, 4.0, (DEVICES, ROWS, TW), jnp.float32)
    random_shifts = jax.random.randint(key_shift, (N_CCD,), H - CM, CM - H + 1).astype(jnp.int32)
    ccd_ids = jnp.arange(N_CCD, dtype=jnp.int32)
    shifts = jnp.where(ccd_ids == 0, CM - H, jnp.where(ccd_ids == 1, H - CM, random_shifts)).astype(jnp.int32)
    tile_view = images.reshape(DEVICES, ROWS // TR, TR, TW // TC, TC).transpose(0, 1, 3, 2, 4).reshape(DEVICES * TILES, TR, TC)
    destination = (owners * TILES + slots).reshape(-1).astype(jnp.int32)
    inverse = jnp.argsort(destination, stable=True).astype(jnp.int32)
    store = jnp.take(tile_view, inverse, axis=0)
    total_rows = N_STRIP * ROWS
    ccd_images = images.reshape(N_CCD, total_rows, TW)
    padded = jnp.pad(ccd_images, ((0, 0), (H, H), (0, 0)))

    def one_ccd(padded_one, shift_one):
        window = lax.dynamic_slice_in_dim(padded_one, CM + shift_one - H, COLS + 2 * H, 1)
        return (gaussian_smooth(window, 1.3, total_rows, COLS), gaussian_smooth(window, 2.4, total_rows, COLS))
    sharp, broad = jax.vmap(one_ccd)(padded, shifts)
    horizontal_pos = 2.0 * (jnp.arange(COLS).astype(jnp.float32) + 0.5) / COLS - 1.0
    vertical_pos = 2.0 * (jnp.arange(total_rows).astype(jnp.float32) + 0.5) / total_rows - 1.0
    horizontal_grid = horizontal_pos[None, None, :]
    vertical_grid = vertical_pos[None, :, None]
    mixing = 0.5 + 0.3 * horizontal_grid + 0.3 * vertical_grid
    background = 0.4 + 0.3 * horizontal_grid - 0.2 * vertical_grid + 0.2 * horizontal_grid * vertical_grid
    noise = jax.random.truncated_normal(key_noise, -4.0, 4.0, (N_CCD, total_rows, COLS), jnp.float32)
    science = mixing * sharp + (1.0 - mixing) * broad + background + 0.3 * noise
    return (store, owners, slots, shifts, science.reshape(DEVICES * ROWS, COLS))


def draw_tile_store(key, part):
    return shared_draw(key)[0]


def draw_tile_source(key, part):
    return shared_draw(key)[1]


def draw_tile_slot(key, part):
    return shared_draw(key)[2]


def draw_shift_cols(key, part):
    return shared_draw(key)[3]


def draw_science(key, part):
    return shared_draw(key)[4]


def set_ends(drawn, stream_key, low, top_value):
    longest = drawn.shape.index(max(drawn.shape))
    spots = []
    for shift in (0, 1):
        where = [jax.random.randint(jax.random.fold_in(stream_key, axis), (), 0, length) for axis, length in enumerate(drawn.shape)]
        where[longest] = (where[longest] + shift) % drawn.shape[longest]
        spots.append(tuple(where))
    return drawn.at[spots[0]].set(low).at[spots[1]].set(top_value)


def setup_inputs(seed: int = 0) -> dict:
    streams_of = jax.random.split(jax.random.key(seed), 7)
    tile_store = draw_tile_store(jax.random.fold_in(streams_of[6], 71), 0)
    tile_source = draw_tile_source(jax.random.fold_in(streams_of[6], 71), 0)
    tile_slot = draw_tile_slot(jax.random.fold_in(streams_of[6], 71), 0)
    shift_cols = draw_shift_cols(jax.random.fold_in(streams_of[6], 71), 0)
    spatial_order = set_ends(jax.random.randint(streams_of[4], (N_CCD,), 0, 3), jax.random.fold_in(streams_of[4], 1), 0, 2).astype(jnp.int32)
    science = draw_science(jax.random.fold_in(streams_of[6], 71), 0)
    return dict(tile_store=tile_store, tile_source=tile_source, tile_slot=tile_slot, shift_cols=shift_cols, spatial_order=spatial_order, science=science)


gauss_sigmas = (0.7, 1.5, 3.0)
poly_degrees = (4, 2, 2)
mono_degrees = (0, 1, 1, 2, 2, 2)
ridge_weight = 0.05

def tap_table(half_width):
    offsets = jnp.arange(-half_width, half_width + 1).astype(jnp.float32)
    table_rows = []
    for sigma_value, top_degree in zip(gauss_sigmas, poly_degrees):
        envelope = jnp.exp(-offsets * offsets / (2.0 * sigma_value * sigma_value))
        envelope_sum = jnp.sum(envelope)
        for power_of in range(top_degree + 1):
            table_rows.append(envelope * (offsets / sigma_value) ** power_of / envelope_sum)
    return jnp.stack(table_rows)

def band_tables(tap_rows, half_width, block_rows):
    tap_count = 2 * half_width + 1
    out_pos = jnp.arange(block_rows)[:, None]
    in_pos = jnp.arange(block_rows + 2 * half_width)[None, :]
    onehot = ((in_pos - out_pos)[:, :, None] == jnp.arange(tap_count)[None, None, :]).astype(jnp.float32)
    band_rows = []
    first_row = 0
    for top_degree in poly_degrees:
        group_taps = tap_rows[first_row:first_row + top_degree + 1]
        band_rows.append(jnp.einsum('rka,ja->jrk', onehot, group_taps, precision=lax.Precision.HIGHEST).astype(jnp.bfloat16))
        first_row += top_degree + 1
    return band_rows

def horizontal_pass(window, tap_rows, out_cols):
    outputs = []
    tap_count = tap_rows.shape[1]
    for filter_id in range(tap_rows.shape[0]):
        taps_now = tap_rows[filter_id]

        def add_tap(tap_id, running, taps_now=taps_now):
            return running + taps_now[tap_id] * lax.dynamic_slice_in_dim(window, tap_id, out_cols, 1)
        summed = lax.fori_loop(0, tap_count, add_tap, jnp.zeros((window.shape[0], out_cols), jnp.float32))
        outputs.append(summed.astype(jnp.bfloat16))
    groups = []
    first_row = 0
    for top_degree in poly_degrees:
        groups.append(jnp.stack(outputs[first_row:first_row + top_degree + 1]))
        first_row += top_degree + 1
    return groups

def block_basis(groups, band_rows, start_row, block_rows, half_width):
    pieces = []
    for group_id, top_degree in enumerate(poly_degrees):
        rows_in = lax.dynamic_slice_in_dim(groups[group_id], start_row, block_rows + 2 * half_width, 1)
        mixed = jnp.einsum('jrk,ikx->ijrx', band_rows[group_id].astype(jnp.float32), rows_in.astype(jnp.float32), precision=lax.Precision.HIGHEST).astype(jnp.bfloat16)
        for horiz_degree in range(top_degree + 1):
            pieces.append(mixed[horiz_degree, :top_degree + 1 - horiz_degree])
    return jnp.concatenate(pieces, axis=0)

def monomials(first_row, block_rows, total_rows, col_count):
    row_pos = (first_row + jnp.arange(block_rows)).astype(jnp.float32)
    vertical_pos = 2.0 * (row_pos + 0.5) / total_rows - 1.0
    horizontal_pos = 2.0 * (jnp.arange(col_count).astype(jnp.float32) + 0.5) / col_count - 1.0
    vertical_grid = jnp.broadcast_to(vertical_pos[:, None], (block_rows, col_count))
    horizontal_grid = jnp.broadcast_to(horizontal_pos[None, :], (block_rows, col_count))
    ones_grid = jnp.ones((block_rows, col_count), jnp.float32)
    return jnp.stack([ones_grid, horizontal_grid, vertical_grid, horizontal_grid * horizontal_grid, horizontal_grid * vertical_grid, vertical_grid * vertical_grid])

def design_rows(basis_block, mono_grid):
    kernel_part = (basis_block.astype(jnp.float32)[:, None] * mono_grid[None]).astype(jnp.bfloat16)
    kernel_part = kernel_part.reshape(basis_block.shape[0] * mono_grid.shape[0], -1)
    back_part = mono_grid.astype(jnp.bfloat16).reshape(mono_grid.shape[0], -1)
    return jnp.concatenate([kernel_part, back_part], axis=0)

def solve_kernel(gram_total, rhs_total, order_value, basis_count):
    degree_list = jnp.array(mono_degrees, dtype=jnp.int32)
    kernel_on = (degree_list <= order_value.astype(jnp.int32)).astype(jnp.float32)
    active = jnp.concatenate([jnp.tile(kernel_on, basis_count), jnp.ones((len(mono_degrees),), jnp.float32)])
    masked = gram_total * active[:, None] * active[None, :] + jnp.diag(1.0 - active)
    system = masked + ridge_weight * jnp.diag(jnp.diag(masked))
    lower = jnp.linalg.cholesky(system)
    middle = jax.scipy.linalg.solve_triangular(lower, rhs_total * active, lower=True)
    return jax.scipy.linalg.solve_triangular(lower.T, middle, lower=False)

def block_difference(basis_block, mono_grid, coeffs, science_block, basis_count):
    spatial_count = mono_grid.shape[0]
    kernel_coef = coeffs[:basis_count * spatial_count].reshape(basis_count, spatial_count)
    back_coef = coeffs[basis_count * spatial_count:]
    weights = jnp.zeros((basis_count,) + mono_grid.shape[1:], jnp.float32)
    background = jnp.zeros(mono_grid.shape[1:], jnp.float32)
    for mono_id in range(spatial_count):
        weights = weights + kernel_coef[:, mono_id, None, None] * mono_grid[mono_id][None]
        background = background + back_coef[mono_id] * mono_grid[mono_id]
    model_image = jnp.sum(basis_block.astype(jnp.float32) * weights, axis=0) + background
    return science_block - model_image

def reference(tile_store, tile_source, tile_slot, shift_cols, spatial_order, science):
    device_count = tile_source.shape[0]
    tile_count = tile_source.shape[1]
    flat_pick = (tile_source.astype(jnp.int32) * tile_count + tile_slot.astype(jnp.int32)).reshape(-1)
    gathered = jnp.take(tile_store, flat_pick, axis=0)
    images = gathered.reshape(device_count, ROWS // TR, TW // TC, TR, TC).transpose(0, 1, 3, 2, 4)
    images = images.reshape(N_CCD, N_STRIP * ROWS, TW)
    total_rows = N_STRIP * ROWS
    science_ccd = science.reshape(N_CCD, total_rows, COLS)
    tap_rows = tap_table(H)
    band_rows = band_tables(tap_rows, H, RB)
    block_count = total_rows // RB
    param_count = NB * NSP + NSP

    def per_ccd(inputs):
        image_rows, science_rows, shift_value, order_value = inputs
        padded = jnp.pad(image_rows, ((H, H), (0, 0)))
        start_col = (CM + shift_value.astype(jnp.int32) - H).astype(jnp.int32)
        window = lax.dynamic_slice_in_dim(padded, start_col, COLS + 2 * H, 1)
        groups = horizontal_pass(window, tap_rows, COLS)

        def gram_step(carry_pair, block_id):
            start_row = (block_id * RB).astype(jnp.int32)
            basis_block = block_basis(groups, band_rows, start_row, RB, H)
            mono_grid = monomials(start_row, RB, total_rows, COLS)
            design = design_rows(basis_block, mono_grid).astype(jnp.float32)
            target = lax.dynamic_slice_in_dim(science_rows, start_row, RB, 0).astype(jnp.bfloat16).astype(jnp.float32).reshape(-1)
            gram_part = jnp.dot(design, design.T, precision=lax.Precision.HIGHEST)
            rhs_part = jnp.dot(design, target, precision=lax.Precision.HIGHEST)
            return ((carry_pair[0] + gram_part, carry_pair[1] + rhs_part), None)
        start_pair = (jnp.zeros((param_count, param_count), jnp.float32), jnp.zeros((param_count,), jnp.float32))
        (gram_total, rhs_total), _ = lax.scan(gram_step, start_pair, jnp.arange(block_count).astype(jnp.int32))
        coeffs = solve_kernel(gram_total, rhs_total, order_value, NB)

        def diff_block(block_id):
            start_row = (block_id * RB).astype(jnp.int32)
            basis_block = block_basis(groups, band_rows, start_row, RB, H)
            mono_grid = monomials(start_row, RB, total_rows, COLS)
            science_block = lax.dynamic_slice_in_dim(science_rows, start_row, RB, 0)
            return block_difference(basis_block, mono_grid, coeffs, science_block, NB)
        return lax.map(diff_block, jnp.arange(block_count).astype(jnp.int32)).reshape(total_rows, COLS)
    result = lax.map(per_ccd, (images, science_ccd, shift_cols, spatial_order))
    return result.reshape(N_CCD * total_rows, COLS)
```

```python
import math

import jax
import jax.numpy as jnp
from jax import lax
from jax.experimental import pallas as pl
from jax.experimental.pallas import tpu as pltpu
from jax.sharding import PartitionSpec as P

H = 11
CM = 128
TW = 2304
LANES = 128
SLOTS = 32

gauss_sigmas = (0.7, 1.5, 3.0)
poly_degrees = (4, 2, 2)
mono_degrees = (0, 1, 1, 2, 2, 2)
mono_powers = ((0, 0), (1, 0), (0, 1), (2, 0), (1, 1), (0, 2))
ridge_weight = 0.05

filters = [(g, n) for g, top in enumerate(poly_degrees) for n in range(top + 1)]
basis_list = [
    (g, i, j) for g, top in enumerate(poly_degrees) for i in range(top + 1) for j in range(top + 1 - i)
]
NB = len(basis_list)
NF = len(filters)
ONE = NB
SCI = NB + 1
moment_keys = [(a, c) for c in range(5) for a in range(5 - c)]
NQ = len(mono_powers)
PIV = 4
VMEM_BYTES = 56 * 1024 * 1024


def envelope_norm(sigma):
    return sum(math.exp(-a * a / (2.0 * sigma * sigma)) for a in range(-H, H + 1))


def iota(shape, dim):
    return lax.broadcasted_iota(jnp.int32, shape, dim)


def split_two(value):
    high = value.astype(jnp.bfloat16)
    low = (value - high.astype(jnp.float32)).astype(jnp.bfloat16)
    return high, low


def pack_kernel(store_ref, source_ref, slot_ref, out_ref):
    me = lax.axis_index("ccd") * lax.axis_size("strip") + lax.axis_index("strip")
    strips, tiles = source_ref.shape
    rows = store_ref.shape[1]

    def one_strip(strip, carry):
        slot = jnp.int32(0)
        for t in range(tiles):
            slot = slot + jnp.where(source_ref[strip, t] == me, slot_ref[strip, t], 0)
        after = lax.rem(strip + 1, strips)
        before = lax.rem(strip + strips - 1, strips)
        out_ref[strip, H : H + rows, :] = store_ref[slot]
        out_ref[after, 0:H, :] = store_ref[slot, rows - H : rows, :]
        out_ref[before, H + rows : 2 * H + rows, :] = store_ref[slot, 0:H, :]
        return carry

    lax.fori_loop(0, strips, one_strip, 0)


def table_kernel(horizontal_high_ref, horizontal_low_ref, vertical_ref, *, rows, high):
    offset = (iota((2 * LANES, LANES), 0) - iota((2 * LANES, LANES), 1) - H).astype(jnp.float32)
    inside = jnp.abs(offset) <= H
    for f, (g, n) in enumerate(filters):
        sigma = gauss_sigmas[g]
        tap = jnp.exp(-offset * offset / (2.0 * sigma * sigma)) * (1.0 / envelope_norm(sigma))
        for _ in range(n):
            tap = tap * (offset * (1.0 / sigma))
        tap = jnp.where(inside, tap, 0.0)
        tap_high, tap_low = split_two(tap)
        horizontal_high_ref[:, f * LANES : (f + 1) * LANES] = tap_high
        horizontal_low_ref[:, f * LANES : (f + 1) * LANES] = tap_low
    width = vertical_ref.shape[1]
    slot = iota((SLOTS, width), 0)
    column = iota((SLOTS, width), 1)
    wanted = jnp.full((SLOTS, width), -1, jnp.int32)
    degree = jnp.zeros((SLOTS, width), jnp.int32)
    scale = jnp.ones((SLOTS, width), jnp.float32)
    weight = jnp.zeros((SLOTS, width), jnp.float32)
    for b, (g, i, j) in enumerate(basis_list):
        here = slot == b
        wanted = jnp.where(here, filters.index((g, i)), wanted)
        degree = jnp.where(here, j, degree)
        scale = jnp.where(here, 1.0 / gauss_sigmas[g], scale)
        weight = jnp.where(here, 1.0 / envelope_norm(gauss_sigmas[g]), weight)
    row_in = column - wanted * high
    matched = (row_in >= 0) & (row_in < high)
    for r in range(rows):
        a = row_in - (r + H)
        z = a.astype(jnp.float32) * scale
        tap = jnp.exp(-0.5 * z * z) * weight
        square = z * z
        power = jnp.where(degree == 1, z, jnp.where(degree == 2, square, 1.0))
        power = jnp.where(degree == 3, square * z, jnp.where(degree == 4, square * square, power))
        keep = matched & (jnp.abs(a) <= H)
        vertical_ref[r * SLOTS : (r + 1) * SLOTS, :] = jnp.where(keep, tap * power, 0.0).astype(jnp.bfloat16)


def u_row(cols):
    return 2.0 * (iota((1, cols), 1).astype(jnp.float32) + 0.5) / cols - 1.0


def basis_kernel(
    arrived_ref, source_ref, shift_ref, science_ref, high_ref, low_ref, vertical_ref,
    basis_out_ref, moment_ref, filtered_ref, basis_ref, sem,
):
    strip_count = lax.axis_size("strip")
    strip = lax.axis_index("strip")
    me = lax.axis_index("ccd") * strip_count + strip
    rows, cols = science_ref.shape
    high = arrived_ref.shape[1]
    strips, tiles = source_ref.shape
    blocks = cols // LANES
    above = jnp.maximum(me - 1, 0)
    below = jnp.minimum(me + 1, strips - 1)
    row_id = iota((high, LANES), 0)
    lane_id = iota((high, LANES), 1)
    is_above = row_id < H
    is_own = row_id < H + rows
    first_row = jnp.where(strip == 0, H, 0)
    last_row = jnp.where(strip == strip_count - 1, H + rows, 2 * H + rows)
    present = (row_id >= first_row) & (row_id < last_row)
    start = CM - H + shift_ref[0]
    skip = jnp.where(start >= LANES, 1, 0)
    offset = start - skip * LANES
    turn = lax.rem(LANES - offset, LANES)
    stays = lane_id < LANES - offset
    turned = []
    for w in range(blocks + 2):
        t = jnp.minimum(w + skip, tiles - 1)
        tile = jnp.where(
            is_above,
            arrived_ref[source_ref[above, t]],
            jnp.where(is_own, arrived_ref[source_ref[me, t]], arrived_ref[source_ref[below, t]]),
        )
        turned.append(pltpu.roll(jnp.where(present, tile, 0.0), turn, 1))
    window = [split_two(jnp.where(stays, turned[w], turned[w + 1])) for w in range(blocks + 1)]
    left = []
    for w in range(blocks):
        (h0, l0), (h1, l1) = window[w], window[w + 1]
        left.append(jnp.concatenate([h0, h1, l0, l1, h0, h1], axis=1))
    left = jnp.concatenate(left, axis=0)
    right = jnp.concatenate([high_ref[...], high_ref[...], low_ref[...]], axis=0)
    filtered_ref[...] = jnp.dot(left, right, preferred_element_type=jnp.float32)

    slot_id = iota((rows * SLOTS, 2 * LANES), 0) & (SLOTS - 1)
    copies = []
    for pair in range(blocks // 2):
        halves = []
        for w in (2 * pair, 2 * pair + 1):
            halves.append(
                jnp.concatenate(
                    [filtered_ref[w * high : (w + 1) * high, f * LANES : (f + 1) * LANES] for f in range(NF)],
                    axis=0,
                ).astype(jnp.bfloat16)
            )
        block = jnp.dot(
            vertical_ref[...], jnp.concatenate(halves, axis=1), preferred_element_type=jnp.float32
        )
        at = slice(pair * 2 * LANES, (pair + 1) * 2 * LANES)
        science = jnp.broadcast_to(science_ref[:, at][:, None, :], (rows, SLOTS, 2 * LANES))
        science = science.reshape(rows * SLOTS, 2 * LANES)
        block = jnp.where(slot_id == ONE, 1.0, jnp.where(slot_id == SCI, science, block))
        basis_ref[:, at] = block.astype(jnp.bfloat16)
    copy = pltpu.make_async_copy(basis_ref, basis_out_ref, sem)
    copy.start()

    u = u_row(cols)
    square = u * u
    totals = [None] * 5
    for r in range(rows):
        here = basis_ref[r * SLOTS : (r + 1) * SLOTS, :]
        wide = here.astype(jnp.float32)
        design = jnp.concatenate(
            [here, (wide * u).astype(jnp.bfloat16), (wide * square).astype(jnp.bfloat16)], axis=0
        )
        product = lax.dot_general(
            design, design, (((1,), (1,)), ((), ())), preferred_element_type=jnp.float32
        )
        v = 2.0 * ((strip * rows + r).astype(jnp.float32) + 0.5) / (rows * strip_count) - 1.0
        for c in range(5):
            totals[c] = product if totals[c] is None else totals[c] + product
            product = product * v
    placed = []
    for a, c in moment_keys:
        first, second = (a, 0) if a < 3 else (a - 2, 2)
        placed.append(
            totals[c][first * SLOTS : (first + 1) * SLOTS, second * SLOTS : (second + 1) * SLOTS]
        )
    placed.append(jnp.zeros((SLOTS, SLOTS), jnp.float32))
    for p in range(4):
        chunk = jnp.concatenate(placed[4 * p : 4 * p + 4], axis=1)
        for k in range(moment_ref.shape[0]):
            moment_ref[k, p * SLOTS : (p + 1) * SLOTS, :] = chunk
    copy.wait()


def solve_kernel(moment_ref, order_ref, science_ref, basis_any_ref, out_ref, system_ref, basis_ref, sem):
    strip_count = lax.axis_size("strip")
    strip = lax.axis_index("strip")
    rows, cols = science_ref.shape
    copy = pltpu.make_async_copy(basis_any_ref, basis_ref, sem)
    copy.start()
    order = order_ref[0]
    total = moment_ref[0]
    for k in range(1, moment_ref.shape[0]):
        total = total + moment_ref[k]
    lane = iota((SLOTS, LANES), 1)
    lane_slot = lane & (SLOTS - 1)
    lane_group = lane // SLOTS
    row_slot = iota((SLOTS, LANES), 0)

    def active(slot, q):
        return ((slot < NB) & (mono_degrees[q] <= order)) | (slot == ONE)

    def moved(key, to_lane, from_lane):
        at = moment_keys.index(key)
        piece = total[(at // 4) * SLOTS : (at // 4 + 1) * SLOTS, :]
        by = (to_lane - from_lane - (at % 4) * SLOTS) % LANES
        return pltpu.roll(piece, by, 1) if by else piece

    for q, (aq, cq) in enumerate(mono_powers):
        tiles = [jnp.zeros((SLOTS, LANES), jnp.float32) for _ in range(2)]
        for k, (ak, ck) in enumerate(mono_powers):
            keep = (lane_group == k % 4) & active(lane_slot, k)
            tiles[k // 4] = jnp.where(keep, moved((aq + ak, cq + ck), (k % 4) * SLOTS, 0), tiles[k // 4])
        tiles[1] = jnp.where(lane == 2 * SLOTS, moved((aq, cq), 2 * SLOTS, SCI), tiles[1])
        row_on = active(row_slot, q)
        for side in range(2):
            tile = jnp.where(row_on, tiles[side], 0.0)
            if q // 4 == side:
                diagonal = lane == row_slot + (q % 4) * SLOTS
                weight = jnp.where(row_on, tile, 1.0) * (1.0 + ridge_weight)
                tile = jnp.where(diagonal, weight, tile)
            system_ref[q * SLOTS : (q + 1) * SLOTS, side * LANES : (side + 1) * LANES] = tile

    def eliminate(q, carry):
        base = pl.multiple_of(q * SLOTS, SLOTS)
        for p in range(0, NB + 1, PIV):
            whole = system_ref[...]
            around = system_ref[pl.ds(base + (p // 8) * 8, 8), :]
            pivot_rows = [around[p % 8 + i : p % 8 + i + 1, :] for i in range(PIV)]
            left = [
                [jnp.broadcast_to(pivot_rows[i][:, p + j : p + j + 1], (1, LANES)) for j in range(PIV)]
                for i in range(PIV)
            ]
            ready = [list(jnp.split(row, 2, axis=1)) for row in pivot_rows]
            for i in range(PIV):
                inverse = 1.0 / left[i][i]
                left[i] = [x * inverse for x in left[i]]
                ready[i] = [x * inverse for x in ready[i]]
                for k in range(PIV):
                    if k != i:
                        factor = left[k][i]
                        left[k] = [x - factor * y for x, y in zip(left[k], left[i])]
                        ready[k] = [x - factor * y for x, y in zip(ready[k], ready[i])]
            ready = [jnp.concatenate(row, axis=1) for row in ready]
            for j in range(PIV):
                whole = whole - whole_column(system_ref, p + j) * ready[j]
            system_ref[...] = whole
            for i in range(PIV):
                system_ref[pl.ds(base + p + i, 1), :] = ready[i]
        system_ref[...] = pltpu.roll(system_ref[...], 2 * LANES - SLOTS, 1)
        return carry

    def whole_column(ref, at):
        return jnp.broadcast_to(ref[:, at : at + 1], ref.shape)

    lax.fori_loop(0, NQ, eliminate, 0)
    solved = system_ref[:, 0:1]
    turned = []
    for q in range(NQ):
        part = solved[q * SLOTS : (q + 1) * SLOTS]
        part = jnp.broadcast_to(jnp.concatenate([part] * (LANES // SLOTS), axis=0), (LANES, LANES))
        turned.append(jnp.transpose(part)[0:rows, :])
    row = iota((rows, LANES), 0)
    v = 2.0 * ((strip * rows + row).astype(jnp.float32) + 0.5) / (rows * strip_count) - 1.0
    group = iota((rows, LANES), 1) // SLOTS
    weights = [jnp.zeros((rows, LANES), jnp.float32) for _ in range(3)]
    for q, (a, c) in enumerate(mono_powers):
        weights[a] = weights[a] + turned[q] * (v * v if c == 2 else v if c else jnp.ones_like(v))
    spread = jnp.concatenate(
        [
            jnp.concatenate(
                [jnp.where(group + m * (LANES // SLOTS) == row, w, 0.0) for m in range(rows * SLOTS // LANES)],
                axis=1,
            )
            for w in weights
        ],
        axis=0,
    )
    spread_high, spread_low = split_two(spread)
    spread = jnp.concatenate([spread_high, spread_low], axis=0)
    copy.wait()
    sums = jnp.dot(spread, basis_ref[...], preferred_element_type=jnp.float32)
    u = u_row(cols)
    model = [sums[a * rows : (a + 1) * rows] + sums[(a + 3) * rows : (a + 4) * rows] for a in range(3)]
    out_ref[...] = science_ref[...] - (model[0] + u * (model[1] + u * model[2]))


def body(tile_store, tile_source, tile_slot, shift_cols, spatial_order, science):
    strip_count = lax.axis_size("strip")
    device_count = lax.axis_size("ccd") * strip_count
    rows, cols = science.shape
    high = -(-(rows + 2 * H) // 8) * 8
    vmem = pl.BlockSpec(memory_space=pltpu.VMEM)
    smem = pl.BlockSpec(memory_space=pltpu.SMEM)
    hbm = pl.BlockSpec(memory_space=pl.ANY)
    params = pltpu.CompilerParams(vmem_limit_bytes=VMEM_BYTES)

    outgoing = pl.pallas_call(
        pack_kernel,
        out_shape=jax.ShapeDtypeStruct((device_count, high, LANES), jnp.float32),
        in_specs=[vmem, smem, smem],
        out_specs=vmem,
        compiler_params=params,
        name="pack",
    )(tile_store, tile_source, tile_slot)
    arrived = lax.all_to_all(outgoing, ("ccd", "strip"), split_axis=0, concat_axis=0, tiled=True)

    taps_high, taps_low, vertical = pl.pallas_call(
        lambda *refs: table_kernel(*refs, rows=rows, high=high),
        out_shape=(
            jax.ShapeDtypeStruct((2 * LANES, NF * LANES), jnp.bfloat16),
            jax.ShapeDtypeStruct((2 * LANES, NF * LANES), jnp.bfloat16),
            jax.ShapeDtypeStruct((rows * SLOTS, NF * high), jnp.bfloat16),
        ),
        out_specs=(vmem, vmem, vmem),
        compiler_params=params,
        name="tables",
        cost_estimate=pl.CostEstimate(flops=10_000_000, bytes_accessed=2_000_000, transcendentals=1_000_000),
    )()

    basis, moments = pl.pallas_call(
        basis_kernel,
        out_shape=(
            jax.ShapeDtypeStruct((rows * SLOTS, cols), jnp.bfloat16),
            jax.ShapeDtypeStruct((strip_count, 4 * SLOTS, LANES), jnp.float32),
        ),
        in_specs=[vmem, smem, smem, vmem, vmem, vmem, vmem],
        out_specs=(hbm, vmem),
        scratch_shapes=[
            pltpu.VMEM((cols // LANES * high, NF * LANES), jnp.float32),
            pltpu.VMEM((rows * SLOTS, cols), jnp.bfloat16),
            pltpu.SemaphoreType.DMA,
        ],
        compiler_params=params,
        name="basis",
    )(arrived, tile_source, shift_cols, science, taps_high, taps_low, vertical)
    gathered = lax.all_to_all(moments, "strip", split_axis=0, concat_axis=0, tiled=True)

    return pl.pallas_call(
        solve_kernel,
        out_shape=jax.ShapeDtypeStruct((rows, cols), jnp.float32),
        in_specs=[vmem, smem, vmem, hbm],
        out_specs=vmem,
        scratch_shapes=[
            pltpu.VMEM((NQ * SLOTS, 2 * LANES), jnp.float32),
            pltpu.VMEM((rows * SLOTS, cols), jnp.bfloat16),
            pltpu.SemaphoreType.DMA,
        ],
        compiler_params=params,
        name="solve",
    )(gathered, spatial_order, science, basis)


def solution(mesh):
    placed = (
        P(("ccd", "strip"), None, None),
        P(),
        P(),
        P("ccd"),
        P("ccd"),
        P(("ccd", "strip"), None),
    )
    return jax.shard_map(
        body, mesh=mesh, in_specs=placed, out_specs=P(("ccd", "strip"), None), check_vma=False
    )
```

```python
import math

import jax
import jax.numpy as jnp
from jax import lax
from jax.experimental import pallas as pl
from jax.experimental.pallas import tpu as pltpu
from jax.sharding import PartitionSpec as P

H = 11
CM = 128
TW = 2304
LANES = 128
SLOTS = 32

gauss_sigmas = (0.7, 1.5, 3.0)
poly_degrees = (4, 2, 2)
mono_degrees = (0, 1, 1, 2, 2, 2)
mono_powers = ((0, 0), (1, 0), (0, 1), (2, 0), (1, 1), (0, 2))
ridge_weight = 0.05

filters = [(g, n) for g, top in enumerate(poly_degrees) for n in range(top + 1)]
basis_list = [
    (g, i, j) for g, top in enumerate(poly_degrees) for i in range(top + 1) for j in range(top + 1 - i)
]
NB = len(basis_list)
NF = len(filters)
ONE = NB
SCI = NB + 1
moment_keys = [(a, c) for c in range(5) for a in range(5 - c)]
NQ = len(mono_powers)


def envelope_norm(sigma):
    return sum(math.exp(-a * a / (2.0 * sigma * sigma)) for a in range(-H, H + 1))


def iota(shape, dim):
    return lax.broadcasted_iota(jnp.int32, shape, dim)


def split_two(value):
    high = value.astype(jnp.bfloat16)
    low = (value - high.astype(jnp.float32)).astype(jnp.bfloat16)
    return high, low


def pack_kernel(store_hbm_ref, source_hbm_ref, slot_hbm_ref, out_ref, store_ref, source_ref, slot_ref, sems):
    pairs = ((source_hbm_ref, source_ref), (slot_hbm_ref, slot_ref), (store_hbm_ref, store_ref))
    copies = [pltpu.make_async_copy(here, there, sems.at[n]) for n, (here, there) in enumerate(pairs)]
    for copy in copies:
        copy.start()
    me = lax.axis_index("ccd") * lax.axis_size("strip") + lax.axis_index("strip")
    copies[0].wait()
    copies[1].wait()
    source = source_ref[...]
    slots = jnp.sum(jnp.where(source == me, slot_ref[...], 0), axis=0, keepdims=True)
    copies[2].wait()
    for strip in range(out_ref.shape[0]):
        out_ref[strip] = store_ref[slots[0, strip]]


def window_kernel(arrived_ref, owner_ref, shift_ref, window_ref, partner_ref, other_ref):
    even = lax.rem(lax.axis_index("strip"), 2) == 0
    tiles = owner_ref.shape[0]
    rows = arrived_ref.shape[1]
    count = window_ref.shape[1] // LANES
    start = CM - H + shift_ref[0]
    skip = start >= LANES
    offset = start - jnp.where(skip, LANES, 0)
    turn = lax.rem(LANES - offset, LANES)
    stays = iota((rows, LANES), 1) < LANES - offset
    owners = owner_ref[...]
    owners = [owners[t, 0] for t in range(tiles)]
    turned = []
    for w in range(count + 1):
        owner = jnp.where(skip, owners[min(w + 1, tiles - 1)], owners[w])
        turned.append(pltpu.roll(arrived_ref[owner], turn, 1))
    for w in range(count):
        tile = jnp.where(stays, turned[w], turned[w + 1])
        window_ref[:, w * LANES : (w + 1) * LANES] = tile
        last, first = tile[rows - H :], tile[:H]
        partner_ref[w * H : (w + 1) * H, :] = jnp.where(even, last, first)
        other_ref[w * H : (w + 1) * H, :] = jnp.where(even, first, last)
    spare = partner_ref.shape[0] - count * H
    partner_ref[count * H :, :] = jnp.zeros((spare, LANES), jnp.float32)
    other_ref[count * H :, :] = jnp.zeros((spare, LANES), jnp.float32)


def table_kernel(source_ref, owner_ref, horizontal_high_ref, horizontal_low_ref, vertical_ref, *, rows, halo):
    me = lax.axis_index("ccd") * lax.axis_size("strip") + lax.axis_index("strip")
    source = source_ref[...]
    owner = jnp.sum(jnp.where(iota(source.shape, 1) == me, source, 0), axis=1, keepdims=True)
    owner_ref[...] = jnp.broadcast_to(owner, owner_ref.shape)
    offset = (iota((2 * LANES, LANES), 0) - iota((2 * LANES, LANES), 1) - H).astype(jnp.float32)
    inside = jnp.abs(offset) <= H
    for f, (g, n) in enumerate(filters):
        sigma = gauss_sigmas[g]
        tap = jnp.exp(-offset * offset / (2.0 * sigma * sigma)) * (1.0 / envelope_norm(sigma))
        for _ in range(n):
            tap = tap * (offset * (1.0 / sigma))
        tap = jnp.where(inside, tap, 0.0)
        tap_high, tap_low = split_two(tap)
        horizontal_high_ref[:, f * LANES : (f + 1) * LANES] = tap_high
        horizontal_low_ref[:, f * LANES : (f + 1) * LANES] = tap_low
    width = vertical_ref.shape[1]
    slot = iota((SLOTS, width), 0)
    column = iota((SLOTS, width), 1)
    wanted = jnp.full((SLOTS, width), -1, jnp.int32)
    degree = jnp.zeros((SLOTS, width), jnp.int32)
    scale = jnp.ones((SLOTS, width), jnp.float32)
    weight = jnp.zeros((SLOTS, width), jnp.float32)
    for b, (g, i, j) in enumerate(basis_list):
        here = slot == b
        wanted = jnp.where(here, filters.index((g, i)), wanted)
        degree = jnp.where(here, j, degree)
        scale = jnp.where(here, 1.0 / gauss_sigmas[g], scale)
        weight = jnp.where(here, 1.0 / envelope_norm(gauss_sigmas[g]), weight)
    own = column - wanted * rows
    outside = column - NF * rows - wanted * halo
    is_own = (own >= 0) & (own < rows)
    is_above = (outside >= 0) & (outside < H)
    is_below = (outside >= H) & (outside < 2 * H)
    is_own = is_own & (column < NF * rows)
    row_in = jnp.where(is_own, own + H, jnp.where(is_below, outside + rows, outside))
    matched = is_own | ((column >= NF * rows) & (is_above | is_below))
    for r in range(rows):
        a = row_in - (r + H)
        z = a.astype(jnp.float32) * scale
        tap = jnp.exp(-0.5 * z * z) * weight
        square = z * z
        power = jnp.where(degree == 1, z, jnp.where(degree == 2, square, 1.0))
        power = jnp.where(degree == 3, square * z, jnp.where(degree == 4, square * square, power))
        keep = matched & (jnp.abs(a) <= H)
        vertical_ref[r * SLOTS : (r + 1) * SLOTS, :] = jnp.where(keep, tap * power, 0.0).astype(jnp.bfloat16)


def wide_tile(value):
    return jnp.concatenate([value, jnp.zeros((value.shape[0], LANES - value.shape[1]), value.dtype)], axis=1)


def turn_lanes(value, by):
    if value.shape[1] < LANES:
        value = wide_tile(value)
    return pltpu.roll(value, by % LANES, 1) if by % LANES else value


def u_row(cols):
    return 2.0 * (iota((1, cols), 1).astype(jnp.float32) + 0.5) / cols - 1.0


def filter_rows(padded, high_ref, low_ref, filtered_ref, out_ref):
    count = padded.shape[0]
    blocks = filtered_ref.shape[0] // count
    window = [split_two(padded[:, w * LANES : (w + 1) * LANES]) for w in range(blocks + 1)]
    left = []
    for w in range(blocks):
        (h0, l0), (h1, l1) = window[w], window[w + 1]
        left.append(jnp.concatenate([h0, h1, l0, l1, h0, h1], axis=1))
    left = jnp.concatenate(left, axis=0)
    right = jnp.concatenate([high_ref[...], high_ref[...], low_ref[...]], axis=0)
    filtered_ref[...] = jnp.dot(left, right, preferred_element_type=jnp.float32)
    for w in range(blocks):
        out_ref[:, w * LANES : (w + 1) * LANES] = jnp.concatenate(
            [filtered_ref[w * count : (w + 1) * count, f * LANES : (f + 1) * LANES] for f in range(NF)],
            axis=0,
        ).astype(jnp.bfloat16)


def own_kernel(window_ref, high_ref, low_ref, out_ref, filtered_ref):
    filter_rows(window_ref[...], high_ref, low_ref, filtered_ref, out_ref)


def basis_kernel(
    own_ref, partner_ref, other_ref, science_hbm_ref, high_ref, low_ref, vertical_ref,
    basis_ref, moment_out_ref,
    padded_ref, filtered_ref, outside_ref, science_ref, moment_ref, sems,
):
    strip_count = lax.axis_size("strip")
    strip = lax.axis_index("strip")
    rows, cols = science_ref.shape
    blocks = cols // LANES
    science_copy = pltpu.make_async_copy(science_hbm_ref, science_ref, sems.at[0])
    science_copy.start()
    even = lax.rem(strip, 2) == 0
    padded_ref[2 * H :, :] = jnp.zeros((padded_ref.shape[0] - 2 * H, padded_ref.shape[1]), jnp.float32)
    for w in range(blocks + 1):
        at = slice(w * LANES, (w + 1) * LANES)
        partner, other = partner_ref[w * H : (w + 1) * H, :], other_ref[w * H : (w + 1) * H, :]
        padded_ref[0:H, at] = jnp.where(even, other, partner)
        padded_ref[H : 2 * H, at] = jnp.where(even, partner, other)
    filter_rows(padded_ref[...], high_ref, low_ref, filtered_ref, outside_ref)

    eighth = iota((8, 2 * LANES), 0)
    science_copy.wait()
    for pair in range(blocks // 2):
        at = slice(pair * 2 * LANES, (pair + 1) * 2 * LANES)
        block = jnp.dot(
            vertical_ref[...],
            jnp.concatenate([own_ref[:, at], outside_ref[:, at]], axis=0),
            preferred_element_type=jnp.float32,
        )
        parts = []
        for r in range(rows):
            last = block[(r + 1) * SLOTS - 8 : (r + 1) * SLOTS]
            last = jnp.where(eighth == ONE % 8, 1.0, jnp.where(eighth == SCI % 8, science_ref[r : r + 1, at], last))
            parts += [block[r * SLOTS : (r + 1) * SLOTS - 8], last]
        basis_ref[:, at] = jnp.concatenate(parts, axis=0).astype(jnp.bfloat16)
    u = u_row(cols)
    square = u * u
    totals = [None] * 5
    for r in range(rows):
        here = basis_ref[r * SLOTS : (r + 1) * SLOTS, :]
        wide = here.astype(jnp.float32)
        design = jnp.concatenate(
            [here, (wide * u).astype(jnp.bfloat16), (wide * square).astype(jnp.bfloat16)], axis=0
        )
        product = lax.dot_general(
            design, design, (((1,), (1,)), ((), ())), preferred_element_type=jnp.float32
        )
        v = 2.0 * ((strip * rows + r).astype(jnp.float32) + 0.5) / (rows * strip_count) - 1.0
        for c in range(5):
            totals[c] = product if totals[c] is None else totals[c] + product
            product = product * v
    half = SLOTS // 2
    row = iota((half, LANES), 0)
    lane = iota((half, LANES), 1)
    chunks = [jnp.zeros((half, LANES), jnp.float32) for _ in range(moment_ref.shape[0] // half)]
    for at, (a, c) in enumerate(moment_keys):
        first, second = (a, 0) if a < 3 else (a - 2, 2)
        group = at % 4 * SLOTS
        top = totals[c][first * SLOTS : first * SLOTS + half, :]
        bottom = totals[c][first * SLOTS + half : (first + 1) * SLOTS, :]
        by = group - second * SLOTS
        corner = jnp.where(lane - group - half <= row, turn_lanes(top, by + half), turn_lanes(bottom, by + 1))
        both = jnp.where(lane - group < half, turn_lanes(bottom, by), corner)
        chunks[at // 4] = jnp.where(lane // SLOTS == at % 4, both, chunks[at // 4])
    for p, chunk in enumerate(chunks):
        moment_ref[p * half : (p + 1) * half, :] = chunk
    sends = []
    for k in range(moment_out_ref.shape[0]):
        sends.append(pltpu.make_async_copy(moment_ref, moment_out_ref.at[k], sems.at[1 + k]))
        sends[k].start()
    for send in sends:
        send.wait()


def solve_kernel(
    moment_ref, order_ref, science_hbm_ref, basis_ref, out_ref,
    system_ref, science_ref, sem,
):
    strip_count = lax.axis_size("strip")
    strip = lax.axis_index("strip")
    rows, cols = science_ref.shape
    copy = pltpu.make_async_copy(science_hbm_ref, science_ref, sem)
    copy.start()
    order = order_ref[0]
    total = moment_ref[0]
    for k in range(1, moment_ref.shape[0]):
        total = total + moment_ref[k]
    half = SLOTS // 2
    across = jnp.transpose(jnp.concatenate([total, jnp.zeros((LANES - total.shape[0], LANES), jnp.float32)], axis=0))
    next_across = pltpu.roll(across, LANES - 1, 0)
    half_row = iota((half, LANES), 0)
    half_lane = iota((half, LANES), 1)
    pieces = {}
    for at, key in enumerate(moment_keys):
        here = total[at // 4 * half : (at // 4 + 1) * half, :]
        group, place = at % 4 * SLOTS, at // 4 * half
        first = across[group : group + half, :]
        second = across[group + half : group + SLOTS, :]
        shifted = next_across[group + half : group + SLOTS, :]
        corner = jnp.where(
            half_lane <= half_row, turn_lanes(here, -group - half), turn_lanes(second, -place)
        )
        top = jnp.where(half_lane < half, corner, turn_lanes(first, half - place))
        corner = jnp.where(
            half_lane - half >= half_row, turn_lanes(here, -group - 1), turn_lanes(shifted, half - place)
        )
        bottom = jnp.where(half_lane < half, turn_lanes(here, -group), corner)
        pieces[key] = jnp.concatenate([top, bottom], axis=0)
    lane = iota((SLOTS, LANES), 1)
    lane_slot = lane & (SLOTS - 1)
    lane_group = lane // SLOTS
    row_slot = iota((SLOTS, LANES), 0)

    def active(slot, q):
        return ((slot < NB) & (mono_degrees[q] <= order)) | (slot == ONE)

    def moved(key, to_lane, from_lane):
        return turn_lanes(pieces[key], to_lane - from_lane)

    for q, (aq, cq) in enumerate(mono_powers):
        tiles = [jnp.zeros((SLOTS, LANES), jnp.float32) for _ in range(2)]
        for k, (ak, ck) in enumerate(mono_powers):
            keep = (lane_group == k % 4) & active(lane_slot, k)
            tiles[k // 4] = jnp.where(keep, moved((aq + ak, cq + ck), (k % 4) * SLOTS, 0), tiles[k // 4])
        tiles[1] = jnp.where(lane == 2 * SLOTS, moved((aq, cq), 2 * SLOTS, SCI), tiles[1])
        row_on = active(row_slot, q)
        for side in range(2):
            tile = jnp.where(row_on, tiles[side], 0.0)
            if q // 4 == side:
                diagonal = lane == row_slot + (q % 4) * SLOTS
                weight = jnp.where(row_on, tile, 1.0) * (1.0 + ridge_weight)
                tile = jnp.where(diagonal, weight, tile)
            system_ref[q * SLOTS : (q + 1) * SLOTS, side * LANES : (side + 1) * LANES] = tile

    groups = [
        [system_ref[8 * i : 8 * i + 8, side * LANES : (side + 1) * LANES] for side in range(2)]
        for i in range(NQ * SLOTS // 8)
    ]
    row8 = iota((8, LANES), 0)

    def column(value, at):
        return jnp.broadcast_to(value[:, at : at + 1], (8, LANES))

    def row_of(value, at):
        return jnp.broadcast_to(value[at : at + 1, :], (8, LANES))

    per = SLOTS // 8
    for q in range(NQ):
        side, start = divmod(q * SLOTS, LANES)
        inner = list(range(q * per, (q + 1) * per))
        for block in inner:
            first = 8 * block % LANES
            count = min(8, NB + 1 - 8 * block % SLOTS)
            panel = [column(groups[block][side], first + j) for j in range(count)] + groups[block][side:]
            for k in range(count):
                inverse = 1.0 / row_of(panel[k], k)
                pivot = row8 == k
                factor = jnp.where(pivot, inverse, -panel[k] * inverse)
                for j in range(k + 1, len(panel)):
                    panel[j] = jnp.where(pivot, 0.0, panel[j]) + factor * row_of(panel[j], k)
            ready = panel[count:]
            spread_rows = [[row_of(tile, j) for j in range(count)] for tile in ready]
            groups[block][side:] = ready
            for i in inner:
                if i != block:
                    factors = [column(groups[i][side], first + j) for j in range(count)]
                    for t in range(side, 2):
                        for j in range(count):
                            groups[i][t] = groups[i][t] - factors[j] * spread_rows[t - side][j]
        ahead = list(range((q + 1) * per, (q + 2) * per)) if q + 1 < NQ else []
        for i in ahead:
            factors = [column(groups[i][side], start + j) for j in range(NB + 1)]
            for t in range(side, 2):
                for j in range(NB + 1):
                    groups[i][t] = groups[i][t] - factors[j] * row_of(groups[inner[j // 8]][t], j % 8)
        rest = [i for i in range(len(groups)) if i not in inner and i not in ahead]
        left = jnp.concatenate([groups[i][side] for i in rest], axis=0)
        right = jnp.concatenate([jnp.concatenate([groups[i][t] for i in inner], axis=0) for t in range(side, 2)], axis=1)
        padding = [jnp.zeros((n, right.shape[1]), jnp.float32) for n in (start, LANES - start - SLOTS)]
        right = jnp.concatenate([x for x in (padding[0], right, padding[1]) if x.shape[0]], axis=0)
        change = jnp.dot(left, right, precision=lax.Precision.HIGHEST, preferred_element_type=jnp.float32)
        for n, i in enumerate(rest):
            for t in range(side, 2):
                groups[i][t] = groups[i][t] - change[8 * n : 8 * n + 8, (t - side) * LANES : (t - side + 1) * LANES]
    solved = jnp.concatenate([group[1][:, 2 * SLOTS : 2 * SLOTS + 1] for group in groups], axis=0)
    turned = []
    for q in range(NQ):
        part = solved[q * SLOTS : (q + 1) * SLOTS]
        part = jnp.broadcast_to(jnp.concatenate([part] * (LANES // SLOTS), axis=0), (LANES, LANES))
        turned.append(jnp.transpose(part)[0:rows, :])
    row = iota((rows, LANES), 0)
    v = 2.0 * ((strip * rows + row).astype(jnp.float32) + 0.5) / (rows * strip_count) - 1.0
    group = iota((rows, LANES), 1) // SLOTS
    weights = [jnp.zeros((rows, LANES), jnp.float32) for _ in range(3)]
    for q, (a, c) in enumerate(mono_powers):
        weights[a] = weights[a] + turned[q] * (v * v if c == 2 else v if c else jnp.ones_like(v))
    spread = jnp.concatenate(
        [
            jnp.concatenate(
                [jnp.where(group + m * (LANES // SLOTS) == row, w, 0.0) for m in range(rows * SLOTS // LANES)],
                axis=1,
            )
            for w in weights
        ],
        axis=0,
    )
    spread_high, spread_low = split_two(spread)
    spread = jnp.concatenate([spread_high, spread_low], axis=0)
    copy.wait()
    sums = jnp.dot(spread, basis_ref[...], preferred_element_type=jnp.float32)
    u = u_row(cols)
    model = [sums[a * rows : (a + 1) * rows] + sums[(a + 3) * rows : (a + 4) * rows] for a in range(3)]
    out_ref[...] = science_ref[...] - (model[0] + u * (model[1] + u * model[2]))


def body(tile_store, tile_source, tile_slot, shift_cols, spatial_order, science):
    strip_count = lax.axis_size("strip")
    device_count = lax.axis_size("ccd") * strip_count
    rows, cols = science.shape
    halo = -(-2 * H // 8) * 8
    vmem = pl.BlockSpec(memory_space=pltpu.VMEM)
    smem = pl.BlockSpec(memory_space=pltpu.SMEM)
    hbm = pl.BlockSpec(memory_space=pltpu.HBM)

    def outside(value):
        return pltpu.with_memory_space_constraint(value, pltpu.HBM)

    def kept(value):
        return pltpu.with_memory_space_constraint(value, pltpu.VMEM)

    tile_store, source, slot, science = map(outside, (tile_store, tile_source.T, tile_slot.T, science))

    def params(mib):
        return pltpu.CompilerParams(vmem_limit_bytes=mib * 1024 * 1024)

    outgoing = pl.pallas_call(
        pack_kernel,
        out_shape=jax.ShapeDtypeStruct((device_count,) + tile_store.shape[1:], jnp.float32),
        in_specs=[hbm, hbm, hbm],
        out_specs=vmem,
        scratch_shapes=[
            pltpu.VMEM(tile_store.shape, jnp.float32),
            pltpu.VMEM(source.shape, jnp.int32),
            pltpu.VMEM(slot.shape, jnp.int32),
            pltpu.SemaphoreType.DMA((3,)),
        ],
        compiler_params=params(60),
        name="pack",
    )(tile_store, source, slot)
    arrived = lax.all_to_all(outgoing, ("ccd", "strip"), split_axis=0, concat_axis=0, tiled=True)
    owner, taps_high, taps_low, vertical = pl.pallas_call(
        lambda *refs: table_kernel(*refs, rows=rows, halo=halo),
        out_shape=(
            pltpu.VMEM((tile_source.shape[1], LANES), jnp.int32),
            pltpu.VMEM((2 * LANES, NF * LANES), jnp.bfloat16),
            pltpu.VMEM((2 * LANES, NF * LANES), jnp.bfloat16),
            pltpu.VMEM((rows * SLOTS, NF * (rows + halo)), jnp.bfloat16),
        ),
        in_specs=[vmem],
        out_specs=(vmem, vmem, vmem, vmem),
        compiler_params=params(16),
        name="tables",
        cost_estimate=pl.CostEstimate(flops=10_000_000, bytes_accessed=2_000_000, transcendentals=1_000_000),
    )(source)
    count = cols // LANES + 1
    edge = -(-count * H // 8) * 8
    window, to_partner, to_other = pl.pallas_call(
        window_kernel,
        out_shape=(
            jax.ShapeDtypeStruct((rows, count * LANES), jnp.float32),
            jax.ShapeDtypeStruct((edge, LANES), jnp.float32),
            jax.ShapeDtypeStruct((edge, LANES), jnp.float32),
        ),
        in_specs=[vmem, vmem, smem],
        out_specs=(vmem, vmem, vmem),
        compiler_params=params(16),
        name="window",
    )(arrived, kept(owner), shift_cols)

    def swap(value, start):
        pairs = [(i, i + 1) for i in range(start, strip_count - 1, 2)]
        return lax.ppermute(value, "strip", pairs + [(j, i) for i, j in pairs])

    from_other = swap(to_other, 1)
    from_partner = swap(to_partner, 0)

    filtered_own = pl.pallas_call(
        own_kernel,
        out_shape=pltpu.VMEM((NF * rows, cols), jnp.bfloat16),
        in_specs=[vmem, vmem, vmem],
        out_specs=vmem,
        scratch_shapes=[pltpu.VMEM((cols // LANES * rows, NF * LANES), jnp.float32)],
        compiler_params=params(16),
        name="own",
        cost_estimate=pl.CostEstimate(flops=600_000_000, bytes_accessed=3_000_000, transcendentals=0),
    )(window, kept(taps_high), kept(taps_low))
    half = SLOTS // 2
    packed = -(-len(moment_keys) // 4) * half
    basis, moments = pl.pallas_call(
        basis_kernel,
        out_shape=(
            pltpu.VMEM((rows * SLOTS, cols), jnp.bfloat16),
            pltpu.HBM((strip_count, packed, LANES), jnp.float32),
        ),
        in_specs=[vmem, vmem, vmem, hbm, vmem, vmem, vmem],
        out_specs=(vmem, hbm),
        scratch_shapes=[
            pltpu.VMEM((halo, count * LANES), jnp.float32),
            pltpu.VMEM((cols // LANES * halo, NF * LANES), jnp.float32),
            pltpu.VMEM((NF * halo, cols), jnp.bfloat16),
            pltpu.VMEM((rows, cols), jnp.float32),
            pltpu.VMEM((packed, LANES), jnp.float32),
            pltpu.SemaphoreType.DMA((1 + strip_count,)),
        ],
        compiler_params=params(24),
        name="basis",
    )(kept(filtered_own), from_partner, from_other, science, kept(taps_high), kept(taps_low), kept(vertical))
    gathered = lax.all_to_all(moments, "strip", split_axis=0, concat_axis=0, tiled=True)

    return pl.pallas_call(
        solve_kernel,
        out_shape=jax.ShapeDtypeStruct((rows, cols), jnp.float32),
        in_specs=[vmem, smem, hbm, vmem],
        out_specs=vmem,
        scratch_shapes=[
            pltpu.VMEM((NQ * SLOTS, 2 * LANES), jnp.float32),
            pltpu.VMEM((rows, cols), jnp.float32),
            pltpu.SemaphoreType.DMA,
        ],
        compiler_params=params(16),
        name="solve",
    )(gathered, spatial_order, science, kept(basis))


def solution(mesh):
    placed = (
        P(("ccd", "strip"), None, None),
        P(),
        P(),
        P("ccd"),
        P("ccd"),
        P(("ccd", "strip"), None),
    )
    return jax.shard_map(
        body, mesh=mesh, in_specs=placed, out_specs=P(("ccd", "strip"), None), check_vma=False
    )
```

```python
import math

import jax
import jax.numpy as jnp
from jax import lax
from jax.experimental import pallas as pl
from jax.experimental.pallas import tpu as pltpu
from jax.sharding import PartitionSpec as P

H = 11
CM = 128
TW = 2304
LANES = 128
SLOTS = 32
TAIL = 32

gauss_sigmas = (0.7, 1.5, 3.0)
poly_degrees = (4, 2, 2)
mono_degrees = (0, 1, 1, 2, 2, 2)
mono_powers = ((0, 0), (1, 0), (0, 1), (2, 0), (1, 1), (0, 2))
ridge_weight = 0.05

filters = [(g, n) for g, top in enumerate(poly_degrees) for n in range(top + 1)]
basis_list = [
    (g, i, j) for g, top in enumerate(poly_degrees) for i in range(top + 1) for j in range(top + 1 - i)
]
NF = len(filters)
HALF = SLOTS // 2
filter_sets = [[f for f in filters if f[0] == 0], [f for f in filters if f[0] > 0]]
image_sets = [[b for b in basis_list if b[0] == 0], [b for b in basis_list if b[0] > 0]]
ONE = len(image_sets[0])
SCI = HALF + len(image_sets[1])
moment_keys = [(a, c) for c in range(5) for a in range(5 - c)]
NQ = len(mono_powers)


def envelope_norm(sigma):
    return sum(math.exp(-a * a / (2.0 * sigma * sigma)) for a in range(-H, H + 1))


def iota(shape, dim):
    return lax.broadcasted_iota(jnp.int32, shape, dim)


def split_two(value):
    high = value.astype(jnp.bfloat16)
    low = (value - high.astype(jnp.float32)).astype(jnp.bfloat16)
    return high, low


def pack_kernel(store_hbm_ref, source_hbm_ref, slot_hbm_ref, out_ref, store_ref, source_ref, slot_ref, sems):
    pairs = ((source_hbm_ref, source_ref), (slot_hbm_ref, slot_ref), (store_hbm_ref, store_ref))
    copies = [pltpu.make_async_copy(here, there, sems.at[n]) for n, (here, there) in enumerate(pairs)]
    for copy in copies:
        copy.start()
    me = lax.axis_index("ccd") * lax.axis_size("strip") + lax.axis_index("strip")
    copies[0].wait()
    copies[1].wait()
    source = source_ref[...]
    slots = jnp.sum(jnp.where(source == me, slot_ref[...], 0), axis=0, keepdims=True)
    copies[2].wait()
    for strip in range(out_ref.shape[0]):
        out_ref[strip] = store_ref[slots[0, strip]]


def window_kernel(arrived_ref, owner_ref, shift_ref, window_ref, partner_ref, other_ref):
    even = lax.rem(lax.axis_index("strip"), 2) == 0
    tiles = owner_ref.shape[0]
    rows = arrived_ref.shape[1]
    count = window_ref.shape[1] // LANES
    start = CM - H + shift_ref[0]
    skip = start >= LANES
    offset = start - jnp.where(skip, LANES, 0)
    turn = lax.rem(LANES - offset, LANES)
    stays = iota((rows, LANES), 1) < LANES - offset
    owners = owner_ref[...]
    owners = [owners[t, 0] for t in range(tiles)]
    turned = []
    for w in range(count + 1):
        owner = jnp.where(skip, owners[min(w + 1, tiles - 1)], owners[w])
        turned.append(pltpu.roll(arrived_ref[owner], turn, 1))
    for w in range(count):
        tile = jnp.where(stays, turned[w], turned[w + 1])
        window_ref[:, w * LANES : (w + 1) * LANES] = tile
        last, first = tile[rows - H :], tile[:H]
        partner_ref[w * H : (w + 1) * H, :] = jnp.where(even, last, first)
        other_ref[w * H : (w + 1) * H, :] = jnp.where(even, first, last)
    spare = partner_ref.shape[0] - count * H
    partner_ref[count * H :, :] = jnp.zeros((spare, LANES), jnp.float32)
    other_ref[count * H :, :] = jnp.zeros((spare, LANES), jnp.float32)


def table_kernel(source_ref, owner_ref, band_ref, *vertical_refs, rows, halo):
    me = lax.axis_index("ccd") * lax.axis_size("strip") + lax.axis_index("strip")
    source = source_ref[...]
    owner = jnp.sum(jnp.where(iota(source.shape, 1) == me, source, 0), axis=1, keepdims=True)
    owner_ref[...] = jnp.broadcast_to(owner, owner_ref.shape)
    row = iota((LANES, LANES), 0)
    near = row - iota((LANES, LANES), 1) - H
    far = near + LANES - row + row % TAIL
    for f, (g, n) in enumerate(filters):
        sigma = gauss_sigmas[g]
        at = slice(f * LANES, (f + 1) * LANES)
        parts = []
        for place in (near, far):
            offset = place.astype(jnp.float32)
            tap = jnp.exp(-offset * offset / (2.0 * sigma * sigma)) * (1.0 / envelope_norm(sigma))
            for _ in range(n):
                tap = tap * (offset * (1.0 / sigma))
            parts.append(split_two(jnp.where(jnp.abs(place) <= H, tap, 0.0)))
        (near_high, near_low), (far_high, far_low) = parts
        band_ref[0:LANES, at] = near_high
        band_ref[LANES : 2 * LANES, at] = near_high
        band_ref[2 * LANES : 3 * LANES, at] = near_low
        tail = jnp.where(row < 2 * TAIL, far_high.astype(jnp.float32), far_low.astype(jnp.float32))
        band_ref[3 * LANES :, at] = jnp.where(row < 3 * TAIL, tail, 0.0).astype(jnp.bfloat16)
    for vertical_ref, members, images in zip(vertical_refs, filter_sets, image_sets):
        width = vertical_ref.shape[1]
        slot = iota((HALF, width), 0)
        column = iota((HALF, width), 1)
        wanted = jnp.full((HALF, width), -1, jnp.int32)
        degree = jnp.zeros((HALF, width), jnp.int32)
        scale = jnp.ones((HALF, width), jnp.float32)
        weight = jnp.zeros((HALF, width), jnp.float32)
        for b, (g, i, j) in enumerate(images):
            here = slot == b
            wanted = jnp.where(here, members.index((g, i)), wanted)
            degree = jnp.where(here, j, degree)
            scale = jnp.where(here, 1.0 / gauss_sigmas[g], scale)
            weight = jnp.where(here, 1.0 / envelope_norm(gauss_sigmas[g]), weight)
        edge = len(members) * rows
        own = column - wanted * rows
        outside = column - edge - wanted * halo
        is_own = (own >= 0) & (own < rows) & (column < edge)
        is_above = (outside >= 0) & (outside < H)
        is_below = (outside >= H) & (outside < 2 * H)
        row_in = jnp.where(is_own, own + H, jnp.where(is_below, outside + rows, outside))
        matched = (is_own | ((column >= edge) & (is_above | is_below))) & (wanted >= 0)
        for r in range(rows):
            a = row_in - (r + H)
            z = a.astype(jnp.float32) * scale
            tap = jnp.exp(-0.5 * z * z) * weight
            square = z * z
            power = jnp.where(degree == 1, z, jnp.where(degree == 2, square, 1.0))
            power = jnp.where(degree == 3, square * z, jnp.where(degree == 4, square * square, power))
            keep = matched & (jnp.abs(a) <= H)
            vertical_ref[r * HALF : (r + 1) * HALF, :] = jnp.where(keep, tap * power, 0.0).astype(jnp.bfloat16)


def wide_tile(value):
    return jnp.concatenate([value, jnp.zeros((value.shape[0], LANES - value.shape[1]), value.dtype)], axis=1)


def turn_lanes(value, by):
    if value.shape[1] < LANES:
        value = wide_tile(value)
    return pltpu.roll(value, by % LANES, 1) if by % LANES else value


def u_row(cols):
    return 2.0 * (iota((1, cols), 1).astype(jnp.float32) + 0.5) / cols - 1.0


def filter_rows(padded, band_ref, filtered_ref, out_refs):
    count = padded.shape[0]
    blocks = filtered_ref.shape[0] // count
    lane = iota((count, LANES), 1)
    window, tails = [], []
    for w in range(blocks + 1):
        tile = padded[:, w * LANES : (w + 1) * LANES]
        high, low = split_two(tile)
        window.append((high, low))
        high, low = high.astype(jnp.float32), low.astype(jnp.float32)
        tail = jnp.where(lane < 2 * TAIL, pltpu.roll(low, TAIL, 1), pltpu.roll(high, 2 * TAIL, 1))
        tails.append(jnp.where(lane < TAIL, high, tail).astype(jnp.bfloat16))
    left = []
    for w in range(blocks):
        high, low = window[w]
        left.append(jnp.concatenate([high, low, high, tails[w + 1]], axis=1))
    filtered_ref[...] = jnp.dot(
        jnp.concatenate(left, axis=0), band_ref[...], preferred_element_type=jnp.float32
    )
    for w in range(blocks):
        for out_ref, members in zip(out_refs, filter_sets):
            first = filters.index(members[0])
            out_ref[:, w * LANES : (w + 1) * LANES] = jnp.concatenate(
                [
                    filtered_ref[w * count : (w + 1) * count, f * LANES : (f + 1) * LANES]
                    for f in range(first, first + len(members))
                ],
                axis=0,
            ).astype(jnp.bfloat16)


def own_kernel(window_ref, band_ref, *refs):
    filter_rows(window_ref[...], band_ref, refs[-1], refs[:-1])


def basis_kernel(
    first_own_ref, second_own_ref, partner_ref, other_ref, science_hbm_ref, band_ref, first_ref, second_ref,
    basis_ref, moment_ref,
    padded_ref, filtered_ref, first_outside_ref, second_outside_ref, science_ref, sems,
):
    strip_count = lax.axis_size("strip")
    strip = lax.axis_index("strip")
    rows, cols = science_ref.shape
    blocks = cols // LANES
    science_copy = pltpu.make_async_copy(science_hbm_ref, science_ref, sems.at[0])
    science_copy.start()
    even = lax.rem(strip, 2) == 0
    padded_ref[2 * H :, :] = jnp.zeros((padded_ref.shape[0] - 2 * H, padded_ref.shape[1]), jnp.float32)
    for w in range(blocks + 1):
        at = slice(w * LANES, (w + 1) * LANES)
        partner, other = partner_ref[w * H : (w + 1) * H, :], other_ref[w * H : (w + 1) * H, :]
        padded_ref[0:H, at] = jnp.where(even, other, partner)
        padded_ref[H : 2 * H, at] = jnp.where(even, partner, other)
    filter_rows(padded_ref[...], band_ref, filtered_ref, (first_outside_ref, second_outside_ref))

    eighth = iota((8, 2 * LANES), 0)
    science_copy.wait()
    for pair in range(blocks // 2):
        at = slice(pair * 2 * LANES, (pair + 1) * 2 * LANES)
        one, two = (
            jnp.dot(
                vertical_ref[...],
                jnp.concatenate([own_ref[:, at], outside_ref[:, at]], axis=0),
                preferred_element_type=jnp.float32,
            )
            for vertical_ref, own_ref, outside_ref in (
                (first_ref, first_own_ref, first_outside_ref),
                (second_ref, second_own_ref, second_outside_ref),
            )
        )
        parts = []
        for r in range(rows):
            low, high = r * HALF, (r + 1) * HALF
            parts += [one[low : high - 8], jnp.where(eighth == ONE % 8, 1.0, one[high - 8 : high])]
            parts += [two[low : high - 8], jnp.where(eighth == SCI % 8, science_ref[r : r + 1, at], two[high - 8 : high])]
        basis_ref[:, at] = jnp.concatenate(parts, axis=0).astype(jnp.bfloat16)
    u = u_row(cols)
    square = u * u
    totals = [None] * 5
    for r in range(rows):
        here = basis_ref[r * SLOTS : (r + 1) * SLOTS, :]
        wide = here.astype(jnp.float32)
        once, twice = (wide * u).astype(jnp.bfloat16), (wide * square).astype(jnp.bfloat16)
        product = lax.dot_general(
            jnp.concatenate([here, once, twice], axis=0),
            jnp.concatenate([here, twice], axis=0),
            (((1,), (1,)), ((), ())),
            preferred_element_type=jnp.float32,
        )
        v = 2.0 * ((strip * rows + r).astype(jnp.float32) + 0.5) / (rows * strip_count) - 1.0
        for c in range(5):
            totals[c] = product if totals[c] is None else totals[c] + product
            product = product * v
    half = SLOTS // 2
    row = iota((half, LANES), 0)
    lane = iota((half, LANES), 1)
    chunks = [jnp.zeros((half, LANES), jnp.float32) for _ in range(moment_ref.shape[0] // half)]
    for at, (a, c) in enumerate(moment_keys):
        first, second = (a, 0) if a < 3 else (a - 2, 1)
        group = at % 4 * SLOTS
        top = totals[c][first * SLOTS : first * SLOTS + half, :]
        bottom = totals[c][first * SLOTS + half : (first + 1) * SLOTS, :]
        by = group - second * SLOTS
        corner = jnp.where(lane - group - half <= row, turn_lanes(top, by + half), turn_lanes(bottom, by + 1))
        both = jnp.where(lane - group < half, turn_lanes(bottom, by), corner)
        chunks[at // 4] = jnp.where(lane // SLOTS == at % 4, both, chunks[at // 4])
    for p, chunk in enumerate(chunks):
        moment_ref[p * half : (p + 1) * half, :] = chunk


def solve_kernel(order_ref, science_hbm_ref, basis_ref, *refs):
    out_hbm_ref, system_ref, science_ref, out_ref, sem, sems = refs[-6:]
    strip_count = lax.axis_size("strip")
    strip = lax.axis_index("strip")
    rows, cols = science_ref.shape
    copy = pltpu.make_async_copy(science_hbm_ref, science_ref, sem)
    copy.start()
    order = order_ref[0]
    total = refs[0][...]
    for ref in refs[1:-6]:
        total = total + ref[...]
    half = SLOTS // 2
    across = jnp.transpose(jnp.concatenate([total, jnp.zeros((LANES - total.shape[0], LANES), jnp.float32)], axis=0))
    next_across = pltpu.roll(across, LANES - 1, 0)
    half_row = iota((half, LANES), 0)
    half_lane = iota((half, LANES), 1)
    pieces = {}
    for at, key in enumerate(moment_keys):
        here = total[at // 4 * half : (at // 4 + 1) * half, :]
        group, place = at % 4 * SLOTS, at // 4 * half
        first = across[group : group + half, :]
        second = across[group + half : group + SLOTS, :]
        shifted = next_across[group + half : group + SLOTS, :]
        corner = jnp.where(
            half_lane <= half_row, turn_lanes(here, -group - half), turn_lanes(second, -place)
        )
        top = jnp.where(half_lane < half, corner, turn_lanes(first, half - place))
        corner = jnp.where(
            half_lane - half >= half_row, turn_lanes(here, -group - 1), turn_lanes(shifted, half - place)
        )
        bottom = jnp.where(half_lane < half, turn_lanes(here, -group), corner)
        pieces[key] = jnp.concatenate([top, bottom], axis=0)
    lane = iota((SLOTS, LANES), 1)
    lane_slot = lane & (SLOTS - 1)
    lane_group = lane // SLOTS
    row_slot = iota((SLOTS, LANES), 0)

    def active(slot, q):
        return ((slot < SCI) & (slot != ONE) & (mono_degrees[q] <= order)) | (slot == ONE)

    def moved(key, to_lane, from_lane):
        return turn_lanes(pieces[key], to_lane - from_lane)

    for q, (aq, cq) in enumerate(mono_powers):
        tiles = [jnp.zeros((SLOTS, LANES), jnp.float32) for _ in range(2)]
        for k, (ak, ck) in enumerate(mono_powers):
            keep = (lane_group == k % 4) & active(lane_slot, k)
            tiles[k // 4] = jnp.where(keep, moved((aq + ak, cq + ck), (k % 4) * SLOTS, 0), tiles[k // 4])
        tiles[1] = jnp.where(lane == 2 * SLOTS, moved((aq, cq), 2 * SLOTS, SCI), tiles[1])
        row_on = active(row_slot, q)
        for side in range(2):
            tile = jnp.where(row_on, tiles[side], 0.0)
            if q // 4 == side:
                diagonal = lane == row_slot + (q % 4) * SLOTS
                weight = jnp.where(row_on, tile, 1.0) * (1.0 + ridge_weight)
                tile = jnp.where(diagonal, weight, tile)
            system_ref[q * SLOTS : (q + 1) * SLOTS, side * LANES : (side + 1) * LANES] = tile

    groups = [
        [system_ref[8 * i : 8 * i + 8, side * LANES : (side + 1) * LANES] for side in range(2)]
        for i in range(NQ * SLOTS // 8)
    ]
    row8 = iota((8, LANES), 0)

    def column(value, at):
        return jnp.broadcast_to(value[:, at : at + 1], (8, LANES))

    def added(terms):
        while len(terms) > 1:
            terms = [sum(terms[n + 1 : n + 2], terms[n]) for n in range(0, len(terms), 2)]
        return terms[0]

    def row_of(value, at):
        return jnp.broadcast_to(value[at : at + 1, :], (8, LANES))

    per = SLOTS // 8
    for q in range(NQ):
        side, start = divmod(q * SLOTS, LANES)
        inner = list(range(q * per, (q + 1) * per))
        for block in inner:
            first = 8 * block % LANES
            count = min(8, SCI - 8 * block % SLOTS)
            panel = [column(groups[block][side], first + j) for j in range(count)] + groups[block][side:]
            for k in range(0, count, 2):
                one, two = panel[k], panel[k + 1]
                a, b = row_of(one, k), row_of(two, k)
                c, d = row_of(one, k + 1), row_of(two, k + 1)
                inverse = 1.0 / (a * d - b * c)
                here, after = row8 == k, row8 == k + 1
                first_factor = inverse * jnp.where(here, d, jnp.where(after, -c, two * c - one * d))
                second_factor = inverse * jnp.where(here, -b, jnp.where(after, a, one * b - two * a))
                for j in range(k + 2, len(panel)):
                    old = jnp.where(here | after, 0.0, panel[j])
                    panel[j] = old + (
                        first_factor * row_of(panel[j], k) + second_factor * row_of(panel[j], k + 1)
                    )
            ready = panel[count:]
            spread_rows = [[row_of(tile, j) for j in range(count)] for tile in ready]
            groups[block][side:] = ready
            for i in inner:
                if i != block:
                    factors = [column(groups[i][side], first + j) for j in range(count)]
                    for t in range(side, 2):
                        products = [factors[j] * spread_rows[t - side][j] for j in range(count)]
                        groups[i][t] = groups[i][t] - added(products)
        ahead = list(range((q + 1) * per, (q + 2) * per)) if q + 1 < NQ else []
        for i in ahead:
            factors = [column(groups[i][side], start + j) for j in range(SCI)]
            for t in range(side, 2):
                products = [factors[j] * row_of(groups[inner[j // 8]][t], j % 8) for j in range(SCI)]
                groups[i][t] = groups[i][t] - added(products)
        rest = [i for i in range(len(groups)) if i not in inner and i not in ahead]
        left = jnp.concatenate([groups[i][side] for i in rest], axis=0)
        right = jnp.concatenate([jnp.concatenate([groups[i][t] for i in inner], axis=0) for t in range(side, 2)], axis=1)
        padding = [jnp.zeros((n, right.shape[1]), jnp.float32) for n in (start, LANES - start - SLOTS)]
        right = jnp.concatenate([x for x in (padding[0], right, padding[1]) if x.shape[0]], axis=0)
        change = jnp.dot(left, right, precision=lax.Precision.HIGHEST, preferred_element_type=jnp.float32)
        for n, i in enumerate(rest):
            for t in range(side, 2):
                groups[i][t] = groups[i][t] - change[8 * n : 8 * n + 8, (t - side) * LANES : (t - side + 1) * LANES]
    solved = jnp.concatenate([group[1][:, 2 * SLOTS : 2 * SLOTS + 1] for group in groups], axis=0)
    turned = []
    for q in range(NQ):
        part = solved[q * SLOTS : (q + 1) * SLOTS]
        part = jnp.broadcast_to(jnp.concatenate([part] * (LANES // SLOTS), axis=0), (LANES, LANES))
        turned.append(jnp.transpose(part)[0:rows, :])
    row = iota((rows, LANES), 0)
    v = 2.0 * ((strip * rows + row).astype(jnp.float32) + 0.5) / (rows * strip_count) - 1.0
    group = iota((rows, LANES), 1) // SLOTS
    weights = [jnp.zeros((rows, LANES), jnp.float32) for _ in range(3)]
    for q, (a, c) in enumerate(mono_powers):
        weights[a] = weights[a] + turned[q] * (v * v if c == 2 else v if c else jnp.ones_like(v))
    spread = jnp.concatenate(
        [
            jnp.concatenate(
                [jnp.where(group + m * (LANES // SLOTS) == row, w, 0.0) for m in range(rows * SLOTS // LANES)],
                axis=1,
            )
            for w in weights
        ],
        axis=0,
    )
    spread_high, spread_low = split_two(spread)
    spread = jnp.concatenate([spread_high, spread_low], axis=0)
    copy.wait()
    u = u_row(cols)
    step = cols // sems.shape[0]
    writes = []
    for n in range(sems.shape[0]):
        at = slice(n * step, (n + 1) * step)
        sums = jnp.dot(spread, basis_ref[:, at], preferred_element_type=jnp.float32)
        model = [sums[a * rows : (a + 1) * rows] + sums[(a + 3) * rows : (a + 4) * rows] for a in range(3)]
        out_ref[:, at] = science_ref[:, at] - (model[0] + u[:, at] * (model[1] + u[:, at] * model[2]))
        writes.append(pltpu.make_async_copy(out_ref.at[:, at], out_hbm_ref.at[:, at], sems.at[n]))
        writes[n].start()
    for write in writes:
        write.wait()


def body(tile_store, tile_source, tile_slot, shift_cols, spatial_order, science):
    strip_count = lax.axis_size("strip")
    device_count = lax.axis_size("ccd") * strip_count
    rows, cols = science.shape
    halo = -(-2 * H // 8) * 8
    vmem = pl.BlockSpec(memory_space=pltpu.VMEM)
    smem = pl.BlockSpec(memory_space=pltpu.SMEM)
    hbm = pl.BlockSpec(memory_space=pltpu.HBM)

    def outside(value):
        return pltpu.with_memory_space_constraint(value, pltpu.HBM)

    def kept(value):
        return pltpu.with_memory_space_constraint(value, pltpu.VMEM)

    tile_store, source, slot, science = map(outside, (tile_store, tile_source.T, tile_slot.T, science))

    def params(mib):
        return pltpu.CompilerParams(vmem_limit_bytes=mib * 1024 * 1024)

    outgoing = pl.pallas_call(
        pack_kernel,
        out_shape=jax.ShapeDtypeStruct((device_count,) + tile_store.shape[1:], jnp.float32),
        in_specs=[hbm, hbm, hbm],
        out_specs=vmem,
        scratch_shapes=[
            pltpu.VMEM(tile_store.shape, jnp.float32),
            pltpu.VMEM(source.shape, jnp.int32),
            pltpu.VMEM(slot.shape, jnp.int32),
            pltpu.SemaphoreType.DMA((3,)),
        ],
        compiler_params=params(60),
        name="pack",
    )(tile_store, source, slot)
    arrived = lax.all_to_all(outgoing, ("ccd", "strip"), split_axis=0, concat_axis=0, tiled=True)
    owner, band, *vertical = pl.pallas_call(
        lambda *refs: table_kernel(*refs, rows=rows, halo=halo),
        out_shape=(
            pltpu.VMEM((tile_source.shape[1], LANES), jnp.int32),
            pltpu.VMEM((4 * LANES, NF * LANES), jnp.bfloat16),
        )
        + tuple(pltpu.VMEM((rows * HALF, len(m) * (rows + halo)), jnp.bfloat16) for m in filter_sets),
        in_specs=[vmem],
        out_specs=(vmem,) * 4,
        compiler_params=params(16),
        name="tables",
        cost_estimate=pl.CostEstimate(flops=10_000_000, bytes_accessed=2_000_000, transcendentals=1_000_000),
    )(source)
    count = cols // LANES + 1
    edge = -(-count * H // 8) * 8
    window, to_partner, to_other = pl.pallas_call(
        window_kernel,
        out_shape=(
            jax.ShapeDtypeStruct((rows, count * LANES), jnp.float32),
            jax.ShapeDtypeStruct((edge, LANES), jnp.float32),
            jax.ShapeDtypeStruct((edge, LANES), jnp.float32),
        ),
        in_specs=[vmem, vmem, smem],
        out_specs=(vmem, vmem, vmem),
        compiler_params=params(16),
        name="window",
    )(arrived, kept(owner), shift_cols)

    def swap(value, start):
        pairs = [(i, i + 1) for i in range(start, strip_count - 1, 2)]
        return lax.ppermute(value, "strip", pairs + [(j, i) for i, j in pairs])

    from_other = swap(to_other, 1)
    from_partner = swap(to_partner, 0)

    filtered_own = pl.pallas_call(
        own_kernel,
        out_shape=tuple(pltpu.VMEM((len(m) * rows, cols), jnp.bfloat16) for m in filter_sets),
        in_specs=[vmem, vmem],
        out_specs=(vmem, vmem),
        scratch_shapes=[pltpu.VMEM((cols // LANES * rows, NF * LANES), jnp.float32)],
        compiler_params=params(16),
        name="own",
        cost_estimate=pl.CostEstimate(flops=600_000_000, bytes_accessed=3_000_000, transcendentals=0),
    )(window, kept(band))
    half = SLOTS // 2
    packed = -(-len(moment_keys) // 4) * half
    basis, moments = pl.pallas_call(
        basis_kernel,
        out_shape=(
            pltpu.VMEM((rows * SLOTS, cols), jnp.bfloat16),
            pltpu.VMEM((packed, LANES), jnp.float32),
        ),
        in_specs=[vmem, vmem, vmem, vmem, hbm, vmem, vmem, vmem],
        out_specs=(vmem, vmem),
        scratch_shapes=[
            pltpu.VMEM((halo, count * LANES), jnp.float32),
            pltpu.VMEM((cols // LANES * halo, NF * LANES), jnp.float32),
            pltpu.VMEM((len(filter_sets[0]) * halo, cols), jnp.bfloat16),
            pltpu.VMEM((len(filter_sets[1]) * halo, cols), jnp.bfloat16),
            pltpu.VMEM((rows, cols), jnp.float32),
            pltpu.SemaphoreType.DMA((1,)),
        ],
        compiler_params=params(24),
        name="basis",
    )(*map(kept, filtered_own), from_partner, from_other, science, *map(kept, (band, *vertical)))

    def exchanged(value, step):
        return lax.ppermute(value, "strip", [(i, i ^ step) for i in range(strip_count)])

    moments = moments + exchanged(moments, 1)
    parts = [moments] + [exchanged(moments, step) for step in range(2, strip_count, 2)]

    return pl.pallas_call(
        solve_kernel,
        out_shape=jax.ShapeDtypeStruct((rows, cols), jnp.float32),
        in_specs=[smem, hbm, vmem] + [vmem] * len(parts),
        out_specs=hbm,
        scratch_shapes=[
            pltpu.VMEM((NQ * SLOTS, 2 * LANES), jnp.float32),
            pltpu.VMEM((rows, cols), jnp.float32),
            pltpu.VMEM((rows, cols), jnp.float32),
            pltpu.SemaphoreType.DMA,
            pltpu.SemaphoreType.DMA((4,)),
        ],
        compiler_params=params(16),
        name="solve",
    )(spatial_order, science, kept(basis), *parts)


def solution(mesh):
    placed = (
        P(("ccd", "strip"), None, None),
        P(),
        P(),
        P("ccd"),
        P("ccd"),
        P(("ccd", "strip"), None),
    )
    return jax.shard_map(
        body, mesh=mesh, in_specs=placed, out_specs=P(("ccd", "strip"), None), check_vma=False
    )
```

```python
import math

import jax
import jax.numpy as jnp
from jax import lax
from jax.experimental import pallas as pl
from jax.experimental.pallas import tpu as pltpu
from jax.sharding import PartitionSpec as P

H = 11
CM = 128
TW = 2304
LANES = 128
SLOTS = 32
TAIL = 32
INSIDE = "promise_in_bounds"

gauss_sigmas = (0.7, 1.5, 3.0)
poly_degrees = (4, 2, 2)
mono_degrees = (0, 1, 1, 2, 2, 2)
mono_powers = ((0, 0), (1, 0), (0, 1), (2, 0), (1, 1), (0, 2))
ridge_weight = 0.05

filters = [(g, n) for g, top in enumerate(poly_degrees) for n in range(top + 1)]
basis_list = [
    (g, i, j) for g, top in enumerate(poly_degrees) for i in range(top + 1) for j in range(top + 1 - i)
]
NF = len(filters)
HALF = SLOTS // 2
filter_sets = [[f for f in filters if f[0] == 0], [f for f in filters if f[0] > 0]]
image_sets = [[b for b in basis_list if b[0] == 0], [b for b in basis_list if b[0] > 0]]
ONE = len(image_sets[0])
SCI = HALF + len(image_sets[1])
moment_keys = [(a, c) for c in range(5) for a in range(5 - c)]
NQ = len(mono_powers)


def envelope_norm(sigma):
    return sum(math.exp(-a * a / (2.0 * sigma * sigma)) for a in range(-H, H + 1))


def iota(shape, dim):
    return lax.broadcasted_iota(jnp.int32, shape, dim)


def split_two(value):
    high = value.astype(jnp.bfloat16)
    low = (value - high.astype(jnp.float32)).astype(jnp.bfloat16)
    return high, low


def pack_kernel(store_hbm_ref, source_hbm_ref, slot_hbm_ref, out_ref, store_ref, source_ref, slot_ref, sems):
    pairs = ((source_hbm_ref, source_ref), (slot_hbm_ref, slot_ref), (store_hbm_ref, store_ref))
    copies = [pltpu.make_async_copy(here, there, sems.at[n]) for n, (here, there) in enumerate(pairs)]
    for copy in copies:
        copy.start()
    me = lax.axis_index("ccd") * lax.axis_size("strip") + lax.axis_index("strip")
    copies[0].wait()
    copies[1].wait()
    source = source_ref[...]
    slots = jnp.sum(jnp.where(source == me, slot_ref[...], 0), axis=0, keepdims=True)
    copies[2].wait()
    for strip in range(out_ref.shape[0]):
        out_ref[strip] = store_ref[slots[0, strip]]


def window_kernel(arrived_ref, owner_ref, shift_ref, window_ref, partner_ref, other_ref):
    even = lax.rem(lax.axis_index("strip"), 2) == 0
    tiles = owner_ref.shape[0]
    rows = arrived_ref.shape[1]
    count = window_ref.shape[1] // LANES
    start = CM - H + shift_ref[0]
    skip = start >= LANES
    offset = start - jnp.where(skip, LANES, 0)
    turn = lax.rem(LANES - offset, LANES)
    stays = iota((rows, LANES), 1) < LANES - offset
    owners = owner_ref[...]
    owners = [owners[t, 0] for t in range(tiles)]
    turned = []
    for w in range(count + 1):
        owner = jnp.where(skip, owners[min(w + 1, tiles - 1)], owners[w])
        turned.append(pltpu.roll(arrived_ref[owner], turn, 1))
    for w in range(count):
        tile = jnp.where(stays, turned[w], turned[w + 1])
        window_ref[:, w * LANES : (w + 1) * LANES] = tile
        last, first = tile[rows - H :], tile[:H]
        partner_ref[w * H : (w + 1) * H, :] = jnp.where(even, last, first)
        other_ref[w * H : (w + 1) * H, :] = jnp.where(even, first, last)
    spare = partner_ref.shape[0] - count * H
    partner_ref[count * H :, :] = jnp.zeros((spare, LANES), jnp.float32)
    other_ref[count * H :, :] = jnp.zeros((spare, LANES), jnp.float32)


def table_kernel(source_ref, owner_ref, band_ref, *vertical_refs, rows, halo):
    me = lax.axis_index("ccd") * lax.axis_size("strip") + lax.axis_index("strip")
    source = source_ref[...]
    owner = jnp.sum(jnp.where(iota(source.shape, 1) == me, source, 0), axis=1, keepdims=True)
    owner_ref[...] = jnp.broadcast_to(owner, owner_ref.shape)
    row = iota((LANES, LANES), 0)
    near = row - iota((LANES, LANES), 1) - H
    far = near + LANES - row + row % TAIL
    for f, (g, n) in enumerate(filters):
        sigma = gauss_sigmas[g]
        at = slice(f * LANES, (f + 1) * LANES)
        parts = []
        for place in (near, far):
            offset = place.astype(jnp.float32)
            tap = jnp.exp(-offset * offset / (2.0 * sigma * sigma)) * (1.0 / envelope_norm(sigma))
            for _ in range(n):
                tap = tap * (offset * (1.0 / sigma))
            parts.append(split_two(jnp.where(jnp.abs(place) <= H, tap, 0.0)))
        (near_high, near_low), (far_high, far_low) = parts
        band_ref[0:LANES, at] = near_high
        band_ref[LANES : 2 * LANES, at] = near_high
        band_ref[2 * LANES : 3 * LANES, at] = near_low
        tail = jnp.where(row < 2 * TAIL, far_high.astype(jnp.float32), far_low.astype(jnp.float32))
        band_ref[3 * LANES :, at] = jnp.where(row < 3 * TAIL, tail, 0.0).astype(jnp.bfloat16)
    for vertical_ref, members, images in zip(vertical_refs, filter_sets, image_sets):
        width = vertical_ref.shape[1]
        slot = iota((HALF, width), 0)
        column = iota((HALF, width), 1)
        wanted = jnp.full((HALF, width), -1, jnp.int32)
        degree = jnp.zeros((HALF, width), jnp.int32)
        scale = jnp.ones((HALF, width), jnp.float32)
        weight = jnp.zeros((HALF, width), jnp.float32)
        for b, (g, i, j) in enumerate(images):
            here = slot == b
            wanted = jnp.where(here, members.index((g, i)), wanted)
            degree = jnp.where(here, j, degree)
            scale = jnp.where(here, 1.0 / gauss_sigmas[g], scale)
            weight = jnp.where(here, 1.0 / envelope_norm(gauss_sigmas[g]), weight)
        edge = len(members) * rows
        own = column - wanted * rows
        outside = column - edge - wanted * halo
        is_own = (own >= 0) & (own < rows) & (column < edge)
        is_above = (outside >= 0) & (outside < H)
        is_below = (outside >= H) & (outside < 2 * H)
        row_in = jnp.where(is_own, own + H, jnp.where(is_below, outside + rows, outside))
        matched = (is_own | ((column >= edge) & (is_above | is_below))) & (wanted >= 0)
        for r in range(rows):
            a = row_in - (r + H)
            z = a.astype(jnp.float32) * scale
            tap = jnp.exp(-0.5 * z * z) * weight
            square = z * z
            power = jnp.where(degree == 1, z, jnp.where(degree == 2, square, 1.0))
            power = jnp.where(degree == 3, square * z, jnp.where(degree == 4, square * square, power))
            keep = matched & (jnp.abs(a) <= H)
            vertical_ref[r * HALF : (r + 1) * HALF, :] = jnp.where(keep, tap * power, 0.0).astype(jnp.bfloat16)


def wide_tile(value):
    return jnp.concatenate([value, jnp.zeros((value.shape[0], LANES - value.shape[1]), value.dtype)], axis=1)


def turn_lanes(value, by):
    if value.shape[1] < LANES:
        value = wide_tile(value)
    return pltpu.roll(value, by % LANES, 1) if by % LANES else value


def u_row(cols):
    return 2.0 * (iota((1, cols), 1).astype(jnp.float32) + 0.5) / cols - 1.0


def filter_rows(padded, band_ref, filtered_ref, out_refs):
    count = padded.shape[0]
    blocks = filtered_ref.shape[0] // count
    lane = iota((count, LANES), 1)
    window, tails = [], []
    for w in range(blocks + 1):
        tile = padded[:, w * LANES : (w + 1) * LANES]
        high, low = split_two(tile)
        window.append((high, low))
        high, low = high.astype(jnp.float32), low.astype(jnp.float32)
        tail = jnp.where(lane < 2 * TAIL, pltpu.roll(low, TAIL, 1), pltpu.roll(high, 2 * TAIL, 1))
        tails.append(jnp.where(lane < TAIL, high, tail).astype(jnp.bfloat16))
    left = []
    for w in range(blocks):
        high, low = window[w]
        left.append(jnp.concatenate([high, low, high, tails[w + 1]], axis=1))
    filtered_ref[...] = jnp.dot(
        jnp.concatenate(left, axis=0), band_ref[...], preferred_element_type=jnp.float32
    )
    for w in range(blocks):
        for out_ref, members in zip(out_refs, filter_sets):
            first = filters.index(members[0])
            out_ref[:, w * LANES : (w + 1) * LANES] = jnp.concatenate(
                [
                    filtered_ref[w * count : (w + 1) * count, f * LANES : (f + 1) * LANES]
                    for f in range(first, first + len(members))
                ],
                axis=0,
            ).astype(jnp.bfloat16)


def own_kernel(window_ref, band_ref, *refs):
    filter_rows(window_ref[...], band_ref, refs[-1], refs[:-1])


def basis_kernel(
    first_own_ref, second_own_ref, partner_ref, other_ref, science_hbm_ref, band_ref, first_ref, second_ref,
    basis_ref, moment_ref,
    padded_ref, filtered_ref, first_outside_ref, second_outside_ref, science_ref, sems,
):
    strip_count = lax.axis_size("strip")
    strip = lax.axis_index("strip")
    rows, cols = science_ref.shape
    blocks = cols // LANES
    science_copy = pltpu.make_async_copy(science_hbm_ref, science_ref, sems.at[0])
    science_copy.start()
    even = lax.rem(strip, 2) == 0
    padded_ref[2 * H :, :] = jnp.zeros((padded_ref.shape[0] - 2 * H, padded_ref.shape[1]), jnp.float32)
    for w in range(blocks + 1):
        at = slice(w * LANES, (w + 1) * LANES)
        partner, other = partner_ref[w * H : (w + 1) * H, :], other_ref[w * H : (w + 1) * H, :]
        padded_ref[0:H, at] = jnp.where(even, other, partner)
        padded_ref[H : 2 * H, at] = jnp.where(even, partner, other)
    filter_rows(padded_ref[...], band_ref, filtered_ref, (first_outside_ref, second_outside_ref))

    eighth = iota((8, 2 * LANES), 0)
    science_copy.wait()
    for pair in range(blocks // 2):
        at = slice(pair * 2 * LANES, (pair + 1) * 2 * LANES)
        one, two = (
            jnp.dot(
                vertical_ref[...],
                jnp.concatenate([own_ref[:, at], outside_ref[:, at]], axis=0),
                preferred_element_type=jnp.float32,
            )
            for vertical_ref, own_ref, outside_ref in (
                (first_ref, first_own_ref, first_outside_ref),
                (second_ref, second_own_ref, second_outside_ref),
            )
        )
        parts = []
        for r in range(rows):
            low, high = r * HALF, (r + 1) * HALF
            parts += [one[low : high - 8], jnp.where(eighth == ONE % 8, 1.0, one[high - 8 : high])]
            parts += [two[low : high - 8], jnp.where(eighth == SCI % 8, science_ref[r : r + 1, at], two[high - 8 : high])]
        basis_ref[:, at] = jnp.concatenate(parts, axis=0).astype(jnp.bfloat16)
    u = u_row(cols)
    square = u * u
    totals = [None] * 5
    for r in range(rows):
        here = basis_ref[r * SLOTS : (r + 1) * SLOTS, :]
        wide = here.astype(jnp.float32)
        once, twice = (wide * u).astype(jnp.bfloat16), (wide * square).astype(jnp.bfloat16)
        product = lax.dot_general(
            jnp.concatenate([here, once, twice], axis=0),
            jnp.concatenate([here, twice], axis=0),
            (((1,), (1,)), ((), ())),
            preferred_element_type=jnp.float32,
        )
        v = 2.0 * ((strip * rows + r).astype(jnp.float32) + 0.5) / (rows * strip_count) - 1.0
        for c in range(5):
            totals[c] = product if totals[c] is None else totals[c] + product
            product = product * v
    half = SLOTS // 2
    row = iota((half, LANES), 0)
    lane = iota((half, LANES), 1)
    chunks = [jnp.zeros((half, LANES), jnp.float32) for _ in range(moment_ref.shape[0] // half)]
    for at, (a, c) in enumerate(moment_keys):
        first, second = (a, 0) if a < 3 else (a - 2, 1)
        group = at % 4 * SLOTS
        top = totals[c][first * SLOTS : first * SLOTS + half, :]
        bottom = totals[c][first * SLOTS + half : (first + 1) * SLOTS, :]
        by = group - second * SLOTS
        corner = jnp.where(lane - group - half <= row, turn_lanes(top, by + half), turn_lanes(bottom, by + 1))
        both = jnp.where(lane - group < half, turn_lanes(bottom, by), corner)
        chunks[at // 4] = jnp.where(lane // SLOTS == at % 4, both, chunks[at // 4])
    for p, chunk in enumerate(chunks):
        moment_ref[p * half : (p + 1) * half, :] = chunk


def solve_kernel(order_ref, science_hbm_ref, basis_ref, *refs):
    out_hbm_ref, system_ref, science_ref, out_ref, sem, sems = refs[-6:]
    strip_count = lax.axis_size("strip")
    strip = lax.axis_index("strip")
    rows, cols = science_ref.shape
    copy = pltpu.make_async_copy(science_hbm_ref, science_ref, sem)
    copy.start()
    order = order_ref[0]
    total = refs[0][...]
    for ref in refs[1:-6]:
        total = total + ref[...]
    half = SLOTS // 2
    across = jnp.transpose(jnp.concatenate([total, jnp.zeros((LANES - total.shape[0], LANES), jnp.float32)], axis=0))
    next_across = pltpu.roll(across, LANES - 1, 0)
    half_row = iota((half, LANES), 0)
    half_lane = iota((half, LANES), 1)
    pieces = {}
    for at, key in enumerate(moment_keys):
        here = total[at // 4 * half : (at // 4 + 1) * half, :]
        group, place = at % 4 * SLOTS, at // 4 * half
        first = across[group : group + half, :]
        second = across[group + half : group + SLOTS, :]
        shifted = next_across[group + half : group + SLOTS, :]
        corner = jnp.where(
            half_lane <= half_row, turn_lanes(here, -group - half), turn_lanes(second, -place)
        )
        top = jnp.where(half_lane < half, corner, turn_lanes(first, half - place))
        corner = jnp.where(
            half_lane - half >= half_row, turn_lanes(here, -group - 1), turn_lanes(shifted, half - place)
        )
        bottom = jnp.where(half_lane < half, turn_lanes(here, -group), corner)
        pieces[key] = jnp.concatenate([top, bottom], axis=0)
    lane = iota((SLOTS, LANES), 1)
    lane_slot = lane & (SLOTS - 1)
    lane_group = lane // SLOTS
    row_slot = iota((SLOTS, LANES), 0)

    def active(slot, q):
        return ((slot < SCI) & (slot != ONE) & (mono_degrees[q] <= order)) | (slot == ONE)

    def moved(key, to_lane, from_lane):
        return turn_lanes(pieces[key], to_lane - from_lane)

    for q, (aq, cq) in enumerate(mono_powers):
        tiles = [jnp.zeros((SLOTS, LANES), jnp.float32) for _ in range(2)]
        for k, (ak, ck) in enumerate(mono_powers):
            keep = (lane_group == k % 4) & active(lane_slot, k)
            tiles[k // 4] = jnp.where(keep, moved((aq + ak, cq + ck), (k % 4) * SLOTS, 0), tiles[k // 4])
        tiles[1] = jnp.where(lane == 2 * SLOTS, moved((aq, cq), 2 * SLOTS, SCI), tiles[1])
        row_on = active(row_slot, q)
        for side in range(2):
            tile = jnp.where(row_on, tiles[side], 0.0)
            if q // 4 == side:
                diagonal = lane == row_slot + (q % 4) * SLOTS
                weight = jnp.where(row_on, tile, 1.0) * (1.0 + ridge_weight)
                tile = jnp.where(diagonal, weight, tile)
            system_ref[q * SLOTS : (q + 1) * SLOTS, side * LANES : (side + 1) * LANES] = tile

    groups = [
        [system_ref[8 * i : 8 * i + 8, side * LANES : (side + 1) * LANES] for side in range(2)]
        for i in range(NQ * SLOTS // 8)
    ]
    row8 = iota((8, LANES), 0)

    def column(value, at):
        return jnp.take_along_axis(value, jnp.full((8, LANES), at, jnp.int32), axis=1, mode=INSIDE)

    def added(terms):
        while len(terms) > 1:
            terms = [sum(terms[n + 1 : n + 2], terms[n]) for n in range(0, len(terms), 2)]
        return terms[0]

    def column_far(value, at):
        return jnp.broadcast_to(value[:, at : at + 1], (8, LANES))

    def row_far(value, at):
        return jnp.broadcast_to(value[at : at + 1, :], (8, LANES))

    def row_of(value, at):
        return jnp.take_along_axis(value, jnp.full((8, LANES), at, jnp.int32), axis=0, mode=INSIDE)

    per = SLOTS // 8
    for q in range(NQ):
        side, start = divmod(q * SLOTS, LANES)
        inner = list(range(q * per, (q + 1) * per))
        for block in inner:
            first = 8 * block % LANES
            count = min(8, SCI - 8 * block % SLOTS)
            panel = [column(groups[block][side], first + j) for j in range(count)] + groups[block][side:]
            known = None
            for k in range(0, count, 2):
                one, two = panel[k], panel[k + 1]
                if known is None:
                    known = [row_of(x, i) for i in (k, k + 1) for x in (one, two)]
                a, b, c, d = known
                inverse = 1.0 / (a * d - b * c)
                pairs = [(row_of(x, k), row_of(x, k + 1)) for x in panel]
                first_rest, second_rest = two * c - one * d, one * b - two * a
                if k + 2 < count:
                    known = []
                    for i in (k + 2, k + 3):
                        before, after = row_of(one, i), row_of(two, i)
                        first_here, second_here = after * c - before * d, before * b - after * a
                        for j in (k + 2, k + 3):
                            step = first_here * pairs[j][0] + second_here * pairs[j][1]
                            known.append(row_of(panel[j], i) + inverse * step)
                here, after = row8 == k, row8 == k + 1
                first_factor = inverse * jnp.where(here, d, jnp.where(after, -c, first_rest))
                second_factor = inverse * jnp.where(here, -b, jnp.where(after, a, second_rest))
                for j in range(k + 2, len(panel)):
                    old = jnp.where(here | after, 0.0, panel[j])
                    panel[j] = old + (first_factor * pairs[j][0] + second_factor * pairs[j][1])
            ready = panel[count:]
            spread_rows = [[row_far(tile, j) for j in range(count)] for tile in ready]
            groups[block][side:] = ready
            for i in inner:
                if i != block:
                    factors = [column_far(groups[i][side], first + j) for j in range(count)]
                    for t in range(side, 2):
                        products = [factors[j] * spread_rows[t - side][j] for j in range(count)]
                        groups[i][t] = groups[i][t] - added(products)
        ahead = list(range((q + 1) * per, (q + 2) * per)) if q + 1 < NQ else []
        for i in ahead:
            factors = [column_far(groups[i][side], start + j) for j in range(SCI)]
            for t in range(side, 2):
                products = [factors[j] * row_far(groups[inner[j // 8]][t], j % 8) for j in range(SCI)]
                groups[i][t] = groups[i][t] - added(products)
        rest = [i for i in range(len(groups)) if i not in inner and i not in ahead]
        left = jnp.concatenate([groups[i][side] for i in rest], axis=0)
        right = jnp.concatenate([jnp.concatenate([groups[i][t] for i in inner], axis=0) for t in range(side, 2)], axis=1)
        padding = [jnp.zeros((n, right.shape[1]), jnp.float32) for n in (start, LANES - start - SLOTS)]
        right = jnp.concatenate([x for x in (padding[0], right, padding[1]) if x.shape[0]], axis=0)
        change = jnp.dot(left, right, precision=lax.Precision.HIGHEST, preferred_element_type=jnp.float32)
        for n, i in enumerate(rest):
            for t in range(side, 2):
                groups[i][t] = groups[i][t] - change[8 * n : 8 * n + 8, (t - side) * LANES : (t - side + 1) * LANES]
    solved = jnp.concatenate([group[1][:, 2 * SLOTS : 2 * SLOTS + 1] for group in groups], axis=0)
    turned = []
    for q in range(NQ):
        part = solved[q * SLOTS : (q + 1) * SLOTS]
        part = jnp.broadcast_to(jnp.concatenate([part] * (LANES // SLOTS), axis=0), (LANES, LANES))
        turned.append(jnp.transpose(part)[0:rows, :])
    row = iota((rows, LANES), 0)
    v = 2.0 * ((strip * rows + row).astype(jnp.float32) + 0.5) / (rows * strip_count) - 1.0
    group = iota((rows, LANES), 1) // SLOTS
    weights = [jnp.zeros((rows, LANES), jnp.float32) for _ in range(3)]
    for q, (a, c) in enumerate(mono_powers):
        weights[a] = weights[a] + turned[q] * (v * v if c == 2 else v if c else jnp.ones_like(v))
    spread = jnp.concatenate(
        [
            jnp.concatenate(
                [jnp.where(group + m * (LANES // SLOTS) == row, w, 0.0) for m in range(rows * SLOTS // LANES)],
                axis=1,
            )
            for w in weights
        ],
        axis=0,
    )
    spread_high, spread_low = split_two(spread)
    spread = jnp.concatenate([spread_high, spread_low], axis=0)
    copy.wait()
    u = u_row(cols)
    step = cols // sems.shape[0]
    writes = []
    for n in range(sems.shape[0]):
        at = slice(n * step, (n + 1) * step)
        sums = jnp.dot(spread, basis_ref[:, at], preferred_element_type=jnp.float32)
        model = [sums[a * rows : (a + 1) * rows] + sums[(a + 3) * rows : (a + 4) * rows] for a in range(3)]
        out_ref[:, at] = science_ref[:, at] - (model[0] + u[:, at] * (model[1] + u[:, at] * model[2]))
        writes.append(pltpu.make_async_copy(out_ref.at[:, at], out_hbm_ref.at[:, at], sems.at[n]))
        writes[n].start()
    for write in writes:
        write.wait()


def body(tile_store, tile_source, tile_slot, shift_cols, spatial_order, science):
    strip_count = lax.axis_size("strip")
    device_count = lax.axis_size("ccd") * strip_count
    rows, cols = science.shape
    halo = -(-2 * H // 8) * 8
    vmem = pl.BlockSpec(memory_space=pltpu.VMEM)
    smem = pl.BlockSpec(memory_space=pltpu.SMEM)
    hbm = pl.BlockSpec(memory_space=pltpu.HBM)

    def outside(value):
        return pltpu.with_memory_space_constraint(value, pltpu.HBM)

    def kept(value):
        return pltpu.with_memory_space_constraint(value, pltpu.VMEM)

    tile_store, source, slot, science = map(outside, (tile_store, tile_source.T, tile_slot.T, science))

    def params(mib):
        return pltpu.CompilerParams(vmem_limit_bytes=mib * 1024 * 1024)

    outgoing = pl.pallas_call(
        pack_kernel,
        out_shape=jax.ShapeDtypeStruct((device_count,) + tile_store.shape[1:], jnp.float32),
        in_specs=[hbm, hbm, hbm],
        out_specs=vmem,
        scratch_shapes=[
            pltpu.VMEM(tile_store.shape, jnp.float32),
            pltpu.VMEM(source.shape, jnp.int32),
            pltpu.VMEM(slot.shape, jnp.int32),
            pltpu.SemaphoreType.DMA((3,)),
        ],
        compiler_params=params(60),
        name="pack",
    )(tile_store, source, slot)
    arrived = lax.all_to_all(outgoing, ("ccd", "strip"), split_axis=0, concat_axis=0, tiled=True)
    owner, band, *vertical = pl.pallas_call(
        lambda *refs: table_kernel(*refs, rows=rows, halo=halo),
        out_shape=(
            pltpu.VMEM((tile_source.shape[1], LANES), jnp.int32),
            pltpu.VMEM((4 * LANES, NF * LANES), jnp.bfloat16),
        )
        + tuple(pltpu.VMEM((rows * HALF, len(m) * (rows + halo)), jnp.bfloat16) for m in filter_sets),
        in_specs=[vmem],
        out_specs=(vmem,) * 4,
        compiler_params=params(16),
        name="tables",
        cost_estimate=pl.CostEstimate(flops=10_000_000, bytes_accessed=2_000_000, transcendentals=1_000_000),
    )(source)
    count = cols // LANES + 1
    edge = -(-count * H // 8) * 8
    window, to_partner, to_other = pl.pallas_call(
        window_kernel,
        out_shape=(
            jax.ShapeDtypeStruct((rows, count * LANES), jnp.float32),
            jax.ShapeDtypeStruct((edge, LANES), jnp.float32),
            jax.ShapeDtypeStruct((edge, LANES), jnp.float32),
        ),
        in_specs=[vmem, vmem, smem],
        out_specs=(vmem, vmem, vmem),
        compiler_params=params(16),
        name="window",
    )(arrived, kept(owner), shift_cols)

    def swap(value, start):
        pairs = [(i, i + 1) for i in range(start, strip_count - 1, 2)]
        return lax.ppermute(value, "strip", pairs + [(j, i) for i, j in pairs])

    from_other = swap(to_other, 1)
    from_partner = swap(to_partner, 0)

    filtered_own = pl.pallas_call(
        own_kernel,
        out_shape=tuple(pltpu.VMEM((len(m) * rows, cols), jnp.bfloat16) for m in filter_sets),
        in_specs=[vmem, vmem],
        out_specs=(vmem, vmem),
        scratch_shapes=[pltpu.VMEM((cols // LANES * rows, NF * LANES), jnp.float32)],
        compiler_params=params(16),
        name="own",
        cost_estimate=pl.CostEstimate(flops=600_000_000, bytes_accessed=3_000_000, transcendentals=0),
    )(window, kept(band))
    half = SLOTS // 2
    packed = -(-len(moment_keys) // 4) * half
    basis, moments = pl.pallas_call(
        basis_kernel,
        out_shape=(
            pltpu.VMEM((rows * SLOTS, cols), jnp.bfloat16),
            pltpu.VMEM((packed, LANES), jnp.float32),
        ),
        in_specs=[vmem, vmem, vmem, vmem, hbm, vmem, vmem, vmem],
        out_specs=(vmem, vmem),
        scratch_shapes=[
            pltpu.VMEM((halo, count * LANES), jnp.float32),
            pltpu.VMEM((cols // LANES * halo, NF * LANES), jnp.float32),
            pltpu.VMEM((len(filter_sets[0]) * halo, cols), jnp.bfloat16),
            pltpu.VMEM((len(filter_sets[1]) * halo, cols), jnp.bfloat16),
            pltpu.VMEM((rows, cols), jnp.float32),
            pltpu.SemaphoreType.DMA((1,)),
        ],
        compiler_params=params(24),
        name="basis",
    )(*map(kept, filtered_own), from_partner, from_other, science, *map(kept, (band, *vertical)))

    def exchanged(value, step):
        return lax.ppermute(value, "strip", [(i, i ^ step) for i in range(strip_count)])

    moments = moments + exchanged(moments, 1)
    parts = [moments] + [exchanged(moments, step) for step in range(2, strip_count, 2)]

    return pl.pallas_call(
        solve_kernel,
        out_shape=jax.ShapeDtypeStruct((rows, cols), jnp.float32),
        in_specs=[smem, hbm, vmem] + [vmem] * len(parts),
        out_specs=hbm,
        scratch_shapes=[
            pltpu.VMEM((NQ * SLOTS, 2 * LANES), jnp.float32),
            pltpu.VMEM((rows, cols), jnp.float32),
            pltpu.VMEM((rows, cols), jnp.float32),
            pltpu.SemaphoreType.DMA,
            pltpu.SemaphoreType.DMA((4,)),
        ],
        compiler_params=params(16),
        name="solve",
    )(spatial_order, science, kept(basis), *parts)


def solution(mesh):
    placed = (
        P(("ccd", "strip"), None, None),
        P(),
        P(),
        P("ccd"),
        P("ccd"),
        P(("ccd", "strip"), None),
    )
    return jax.shard_map(
        body, mesh=mesh, in_specs=placed, out_specs=P(("ccd", "strip"), None), check_vma=False
    )
```

```python
import math

import jax
import jax.numpy as jnp
from jax import lax
from jax.experimental import pallas as pl
from jax.experimental.pallas import tpu as pltpu
from jax.sharding import PartitionSpec as P

H = 11
CM = 128
TW = 2304
LANES = 128
SLOTS = 32
TAIL = 32
INSIDE = "promise_in_bounds"

gauss_sigmas = (0.7, 1.5, 3.0)
poly_degrees = (4, 2, 2)
mono_degrees = (0, 1, 1, 2, 2, 2)
mono_powers = ((0, 0), (1, 0), (0, 1), (2, 0), (1, 1), (0, 2))
ridge_weight = 0.05

filters = [(g, n) for g, top in enumerate(poly_degrees) for n in range(top + 1)]
basis_list = [
    (g, i, j) for g, top in enumerate(poly_degrees) for i in range(top + 1) for j in range(top + 1 - i)
]
NF = len(filters)
HALF = SLOTS // 2
filter_sets = [[f for f in filters if f[0] == 0], [f for f in filters if f[0] > 0]]
image_sets = [[b for b in basis_list if b[0] == 0], [b for b in basis_list if b[0] > 0]]
ONE = len(image_sets[0])
SCI = HALF + len(image_sets[1])
moment_keys = [(a, c) for c in range(5) for a in range(5 - c)]
NQ = len(mono_powers)


def envelope_norm(sigma):
    return sum(math.exp(-a * a / (2.0 * sigma * sigma)) for a in range(-H, H + 1))


def iota(shape, dim):
    return lax.broadcasted_iota(jnp.int32, shape, dim)


def split_two(value):
    high = value.astype(jnp.bfloat16)
    low = (value - high.astype(jnp.float32)).astype(jnp.bfloat16)
    return high, low


def pack_kernel(store_hbm_ref, source_hbm_ref, slot_hbm_ref, out_ref, store_ref, source_ref, slot_ref, sems):
    pairs = ((source_hbm_ref, source_ref), (slot_hbm_ref, slot_ref), (store_hbm_ref, store_ref))
    copies = [pltpu.make_async_copy(here, there, sems.at[n]) for n, (here, there) in enumerate(pairs)]
    for copy in copies:
        copy.start()
    me = lax.axis_index("ccd") * lax.axis_size("strip") + lax.axis_index("strip")
    copies[0].wait()
    copies[1].wait()
    source = source_ref[...]
    slots = jnp.sum(jnp.where(source == me, slot_ref[...], 0), axis=0, keepdims=True)
    copies[2].wait()
    for strip in range(out_ref.shape[0]):
        out_ref[strip] = store_ref[slots[0, strip]]


def window_kernel(arrived_ref, owner_ref, shift_ref, window_ref, partner_ref, other_ref):
    even = lax.rem(lax.axis_index("strip"), 2) == 0
    tiles = owner_ref.shape[0]
    rows = arrived_ref.shape[1]
    count = window_ref.shape[1] // LANES
    start = CM - H + shift_ref[0]
    skip = start >= LANES
    offset = start - jnp.where(skip, LANES, 0)
    turn = lax.rem(LANES - offset, LANES)
    stays = iota((rows, LANES), 1) < LANES - offset
    owners = owner_ref[...]
    owners = [owners[t, 0] for t in range(tiles)]
    turned = []
    for w in range(count + 1):
        owner = jnp.where(skip, owners[min(w + 1, tiles - 1)], owners[w])
        turned.append(pltpu.roll(arrived_ref[owner], turn, 1))
    for w in range(count):
        tile = jnp.where(stays, turned[w], turned[w + 1])
        window_ref[:, w * LANES : (w + 1) * LANES] = tile
        last, first = tile[rows - H :], tile[:H]
        partner_ref[w * H : (w + 1) * H, :] = jnp.where(even, last, first)
        other_ref[w * H : (w + 1) * H, :] = jnp.where(even, first, last)
    spare = partner_ref.shape[0] - count * H
    partner_ref[count * H :, :] = jnp.zeros((spare, LANES), jnp.float32)
    other_ref[count * H :, :] = jnp.zeros((spare, LANES), jnp.float32)


def table_kernel(source_ref, science_hbm_ref, owner_ref, science_ref, band_ref, *refs):
    *vertical_refs, sem = refs
    rows = science_ref.shape[0]
    science_copy = pltpu.make_async_copy(science_hbm_ref, science_ref, sem)
    science_copy.start()
    even = lax.rem(lax.axis_index("strip"), 2) == 0
    me = lax.axis_index("ccd") * lax.axis_size("strip") + lax.axis_index("strip")
    source = source_ref[...]
    owner = jnp.sum(jnp.where(iota(source.shape, 1) == me, source, 0), axis=1, keepdims=True)
    owner_ref[...] = jnp.broadcast_to(owner, owner_ref.shape)
    row = iota((LANES, LANES), 0)
    near = row - iota((LANES, LANES), 1) - H
    far = near + LANES - row + row % TAIL
    for f, (g, n) in enumerate(filters):
        sigma = gauss_sigmas[g]
        at = slice(f * LANES, (f + 1) * LANES)
        parts = []
        for place in (near, far):
            offset = place.astype(jnp.float32)
            tap = jnp.exp(-offset * offset / (2.0 * sigma * sigma)) * (1.0 / envelope_norm(sigma))
            for _ in range(n):
                tap = tap * (offset * (1.0 / sigma))
            parts.append(split_two(jnp.where(jnp.abs(place) <= H, tap, 0.0)))
        (near_high, near_low), (far_high, far_low) = parts
        band_ref[0:LANES, at] = near_high
        band_ref[LANES : 2 * LANES, at] = near_high
        band_ref[2 * LANES : 3 * LANES, at] = near_low
        tail = jnp.where(row < 2 * TAIL, far_high.astype(jnp.float32), far_low.astype(jnp.float32))
        band_ref[3 * LANES :, at] = jnp.where(row < 3 * TAIL, tail, 0.0).astype(jnp.bfloat16)
    for vertical_ref, members, images in zip(vertical_refs, filter_sets, image_sets):
        width = vertical_ref.shape[1]
        slot = iota((HALF, width), 0)
        column = iota((HALF, width), 1)
        wanted = jnp.full((HALF, width), -1, jnp.int32)
        degree = jnp.zeros((HALF, width), jnp.int32)
        scale = jnp.ones((HALF, width), jnp.float32)
        weight = jnp.zeros((HALF, width), jnp.float32)
        for b, (g, i, j) in enumerate(images):
            here = slot == b
            wanted = jnp.where(here, members.index((g, i)), wanted)
            degree = jnp.where(here, j, degree)
            scale = jnp.where(here, 1.0 / gauss_sigmas[g], scale)
            weight = jnp.where(here, 1.0 / envelope_norm(gauss_sigmas[g]), weight)
        edge = len(members) * rows
        section = jnp.where(column < edge, 0, jnp.where(column < 2 * edge, 1, 2))
        local = column - section * edge - wanted * rows
        is_own = section == 0
        matched = (local >= 0) & (local < jnp.where(is_own, rows, H)) & (wanted >= 0)
        is_below = (section == 1) == even
        row_in = local + jnp.where(is_own, H, jnp.where(is_below, H + rows, 0))
        for r in range(rows):
            a = row_in - (r + H)
            z = a.astype(jnp.float32) * scale
            tap = jnp.exp(-0.5 * z * z) * weight
            square = z * z
            power = jnp.where(degree == 1, z, jnp.where(degree == 2, square, 1.0))
            power = jnp.where(degree == 3, square * z, jnp.where(degree == 4, square * square, power))
            keep = matched & (jnp.abs(a) <= H)
            vertical_ref[r * HALF : (r + 1) * HALF, :] = jnp.where(keep, tap * power, 0.0).astype(jnp.bfloat16)
    science_copy.wait()


def wide_tile(value):
    return jnp.concatenate([value, jnp.zeros((value.shape[0], LANES - value.shape[1]), value.dtype)], axis=1)


def turn_lanes(value, by):
    if value.shape[1] < LANES:
        value = wide_tile(value)
    return pltpu.roll(value, by % LANES, 1) if by % LANES else value


def u_row(cols):
    return 2.0 * (iota((1, cols), 1).astype(jnp.float32) + 0.5) / cols - 1.0


def filter_rows(padded, band_ref, filtered_ref, out_refs):
    count = padded.shape[0]
    blocks = filtered_ref.shape[0] // count
    lane = iota((count, LANES), 1)
    window, tails = [], []
    for w in range(blocks + 1):
        tile = padded[:, w * LANES : (w + 1) * LANES]
        high, low = split_two(tile)
        window.append((high, low))
        high, low = high.astype(jnp.float32), low.astype(jnp.float32)
        tail = jnp.where(lane < 2 * TAIL, pltpu.roll(low, TAIL, 1), pltpu.roll(high, 2 * TAIL, 1))
        tails.append(jnp.where(lane < TAIL, high, tail).astype(jnp.bfloat16))
    left = []
    for w in range(blocks):
        high, low = window[w]
        left.append(jnp.concatenate([high, low, high, tails[w + 1]], axis=1))
    filtered_ref[...] = jnp.dot(
        jnp.concatenate(left, axis=0), band_ref[...], preferred_element_type=jnp.float32
    )
    for w in range(blocks):
        for out_ref, members in zip(out_refs, filter_sets):
            first = filters.index(members[0])
            out_ref[:, w * LANES : (w + 1) * LANES] = jnp.concatenate(
                [
                    filtered_ref[w * count : (w + 1) * count, f * LANES : (f + 1) * LANES]
                    for f in range(first, first + len(members))
                ],
                axis=0,
            ).astype(jnp.bfloat16)


def own_kernel(window_ref, band_ref, *refs):
    filter_rows(window_ref[...], band_ref, refs[-1], refs[:-1])


def row_split(rows):
    even = lax.rem(lax.axis_index("strip"), 2) == 0
    return (jnp.where(even, H, 0), rows - H), (jnp.where(even, 0, rows - H), H)


def filter_halo(halo_ref, band_ref, padded_ref, filtered_ref, out_refs):
    rows = padded_ref.shape[0]
    padded_ref[H:, :] = jnp.zeros((rows - H, padded_ref.shape[1]), jnp.float32)
    for w in range(padded_ref.shape[1] // LANES):
        padded_ref[0:H, w * LANES : (w + 1) * LANES] = halo_ref[w * H : (w + 1) * H, :]
    filter_rows(padded_ref[...], band_ref, filtered_ref, out_refs)


def images_and_moments(start, count, vertical_refs, source_refs, science_ref, basis_ref):
    strip_count = lax.axis_size("strip")
    strip = lax.axis_index("strip")
    rows, cols = science_ref.shape
    eighth = iota((8, 2 * LANES), 0)
    for pair in range(cols // LANES // 2):
        at = slice(pair * 2 * LANES, (pair + 1) * 2 * LANES)
        blocks = []
        for n, vertical_ref in enumerate(vertical_refs):
            right = jnp.concatenate([refs[n][:, at] for refs in source_refs], axis=0)
            left = vertical_ref[pl.ds(pl.multiple_of(start * HALF, HALF), count * HALF), 0 : right.shape[0]]
            blocks.append(jnp.dot(left, right, preferred_element_type=jnp.float32))
        one, two = blocks
        parts = []
        for r in range(count):
            low, high = r * HALF, (r + 1) * HALF
            science = science_ref[pl.ds(start + r, 1), at]
            parts += [one[low : high - 8], jnp.where(eighth == ONE % 8, 1.0, one[high - 8 : high])]
            parts += [two[low : high - 8], jnp.where(eighth == SCI % 8, science, two[high - 8 : high])]
        basis_ref[:, at] = jnp.concatenate(parts, axis=0).astype(jnp.bfloat16)

    u = u_row(cols)
    square = u * u
    totals = [None] * 5
    for r in range(count):
        here = basis_ref[r * SLOTS : (r + 1) * SLOTS, :]
        wide = here.astype(jnp.float32)
        once, twice = (wide * u).astype(jnp.bfloat16), (wide * square).astype(jnp.bfloat16)
        product = lax.dot_general(
            jnp.concatenate([here, once, twice], axis=0),
            jnp.concatenate([here, twice], axis=0),
            (((1,), (1,)), ((), ())),
            preferred_element_type=jnp.float32,
        )
        v = 2.0 * ((strip * rows + start + r).astype(jnp.float32) + 0.5) / (rows * strip_count) - 1.0
        for c in range(5):
            totals[c] = product if totals[c] is None else totals[c] + product
            product = product * v
    row = iota((HALF, LANES), 0)
    lane = iota((HALF, LANES), 1)
    chunks = [jnp.zeros((HALF, LANES), jnp.float32) for _ in range(-(-len(moment_keys) // 4))]
    for at, (a, c) in enumerate(moment_keys):
        first, second = (a, 0) if a < 3 else (a - 2, 1)
        group = at % 4 * SLOTS
        top = totals[c][first * SLOTS : first * SLOTS + HALF, :]
        bottom = totals[c][first * SLOTS + HALF : (first + 1) * SLOTS, :]
        by = group - second * SLOTS
        corner = jnp.where(lane - group - HALF <= row, turn_lanes(top, by + HALF), turn_lanes(bottom, by + 1))
        both = jnp.where(lane - group < HALF, turn_lanes(bottom, by), corner)
        chunks[at // 4] = jnp.where(lane // SLOTS == at % 4, both, chunks[at // 4])
    return jnp.concatenate(chunks, axis=0)


def early_kernel(
    first_own_ref, second_own_ref, partner_ref, science_ref, band_ref, first_ref, second_ref,
    basis_ref, moment_ref, first_partner_ref, second_partner_ref,
    padded_ref, filtered_ref,
):
    partner_refs = first_partner_ref, second_partner_ref
    filter_halo(partner_ref, band_ref, padded_ref, filtered_ref, partner_refs)
    start, count = row_split(science_ref.shape[0])[0]
    sources = (first_own_ref, second_own_ref), partner_refs
    moment_ref[...] = images_and_moments(start, count, (first_ref, second_ref), sources, science_ref, basis_ref)


def late_kernel(
    first_own_ref, second_own_ref, first_partner_ref, second_partner_ref, other_ref, early_ref,
    science_ref, band_ref, first_ref, second_ref,
    basis_ref, moment_ref,
    padded_ref, filtered_ref, first_other_ref, second_other_ref,
):
    other_refs = first_other_ref, second_other_ref
    filter_halo(other_ref, band_ref, padded_ref, filtered_ref, other_refs)
    start, count = row_split(science_ref.shape[0])[1]
    sources = (first_own_ref, second_own_ref), (first_partner_ref, second_partner_ref), other_refs
    moments = images_and_moments(start, count, (first_ref, second_ref), sources, science_ref, basis_ref)
    moment_ref[...] = early_ref[...] + moments


def solve_kernel(order_ref, science_ref, early_ref, late_ref, *refs):
    out_hbm_ref, system_ref, out_ref, sems = refs[-4:]
    strip_count = lax.axis_size("strip")
    strip = lax.axis_index("strip")
    rows, cols = science_ref.shape
    order = order_ref[0]
    total = refs[0][...]
    for ref in refs[1:-4]:
        total = total + ref[...]
    half = SLOTS // 2
    across = jnp.transpose(jnp.concatenate([total, jnp.zeros((LANES - total.shape[0], LANES), jnp.float32)], axis=0))
    next_across = pltpu.roll(across, LANES - 1, 0)
    half_row = iota((half, LANES), 0)
    half_lane = iota((half, LANES), 1)
    pieces = {}
    for at, key in enumerate(moment_keys):
        here = total[at // 4 * half : (at // 4 + 1) * half, :]
        group, place = at % 4 * SLOTS, at // 4 * half
        first = across[group : group + half, :]
        second = across[group + half : group + SLOTS, :]
        shifted = next_across[group + half : group + SLOTS, :]
        corner = jnp.where(
            half_lane <= half_row, turn_lanes(here, -group - half), turn_lanes(second, -place)
        )
        top = jnp.where(half_lane < half, corner, turn_lanes(first, half - place))
        corner = jnp.where(
            half_lane - half >= half_row, turn_lanes(here, -group - 1), turn_lanes(shifted, half - place)
        )
        bottom = jnp.where(half_lane < half, turn_lanes(here, -group), corner)
        pieces[key] = jnp.concatenate([top, bottom], axis=0)
    lane = iota((SLOTS, LANES), 1)
    lane_slot = lane & (SLOTS - 1)
    lane_group = lane // SLOTS
    row_slot = iota((SLOTS, LANES), 0)

    def active(slot, q):
        return ((slot < SCI) & (slot != ONE) & (mono_degrees[q] <= order)) | (slot == ONE)

    def moved(key, to_lane, from_lane):
        return turn_lanes(pieces[key], to_lane - from_lane)

    for q, (aq, cq) in enumerate(mono_powers):
        tiles = [jnp.zeros((SLOTS, LANES), jnp.float32) for _ in range(2)]
        for k, (ak, ck) in enumerate(mono_powers):
            keep = (lane_group == k % 4) & active(lane_slot, k)
            tiles[k // 4] = jnp.where(keep, moved((aq + ak, cq + ck), (k % 4) * SLOTS, 0), tiles[k // 4])
        tiles[1] = jnp.where(lane == 2 * SLOTS, moved((aq, cq), 2 * SLOTS, SCI), tiles[1])
        row_on = active(row_slot, q)
        for side in range(2):
            tile = jnp.where(row_on, tiles[side], 0.0)
            if q // 4 == side:
                diagonal = lane == row_slot + (q % 4) * SLOTS
                weight = jnp.where(row_on, tile, 1.0) * (1.0 + ridge_weight)
                tile = jnp.where(diagonal, weight, tile)
            system_ref[q * SLOTS : (q + 1) * SLOTS, side * LANES : (side + 1) * LANES] = tile

    groups = [
        [system_ref[8 * i : 8 * i + 8, side * LANES : (side + 1) * LANES] for side in range(2)]
        for i in range(NQ * SLOTS // 8)
    ]
    row8 = iota((8, LANES), 0)

    def column(value, at):
        return jnp.take_along_axis(value, jnp.full((8, LANES), at, jnp.int32), axis=1, mode=INSIDE)

    def added(terms):
        while len(terms) > 1:
            terms = [sum(terms[n + 1 : n + 2], terms[n]) for n in range(0, len(terms), 2)]
        return terms[0]

    def column_far(value, at):
        return jnp.broadcast_to(value[:, at : at + 1], (8, LANES))

    def row_far(value, at):
        return jnp.broadcast_to(value[at : at + 1, :], (8, LANES))

    def row_of(value, at):
        return jnp.take_along_axis(value, jnp.full((8, LANES), at, jnp.int32), axis=0, mode=INSIDE)

    per = SLOTS // 8
    for q in range(NQ):
        side, start = divmod(q * SLOTS, LANES)
        inner = list(range(q * per, (q + 1) * per))
        for block in inner:
            first = 8 * block % LANES
            count = min(8, SCI - 8 * block % SLOTS)
            panel = [column(groups[block][side], first + j) for j in range(count)] + groups[block][side:]
            known = None
            for k in range(0, count, 2):
                one, two = panel[k], panel[k + 1]
                if known is None:
                    known = [row_of(x, i) for i in (k, k + 1) for x in (one, two)]
                a, b, c, d = known
                inverse = 1.0 / (a * d - b * c)
                pairs = [(row_of(x, k), row_of(x, k + 1)) for x in panel]
                first_rest, second_rest = two * c - one * d, one * b - two * a
                if k + 2 < count:
                    known = []
                    for i in (k + 2, k + 3):
                        before, after = row_of(one, i), row_of(two, i)
                        first_here, second_here = after * c - before * d, before * b - after * a
                        for j in (k + 2, k + 3):
                            step = first_here * pairs[j][0] + second_here * pairs[j][1]
                            known.append(row_of(panel[j], i) + inverse * step)
                here, after = row8 == k, row8 == k + 1
                first_factor = inverse * jnp.where(here, d, jnp.where(after, -c, first_rest))
                second_factor = inverse * jnp.where(here, -b, jnp.where(after, a, second_rest))
                for j in range(k + 2, len(panel)):
                    old = jnp.where(here | after, 0.0, panel[j])
                    panel[j] = old + (first_factor * pairs[j][0] + second_factor * pairs[j][1])
            ready = panel[count:]
            spread_rows = [[row_far(tile, j) for j in range(count)] for tile in ready]
            groups[block][side:] = ready
            for i in inner:
                if i != block:
                    factors = [column_far(groups[i][side], first + j) for j in range(count)]
                    for t in range(side, 2):
                        products = [factors[j] * spread_rows[t - side][j] for j in range(count)]
                        groups[i][t] = groups[i][t] - added(products)
        ahead = list(range((q + 1) * per, (q + 2) * per)) if q + 1 < NQ else []
        for i in ahead:
            factors = [column_far(groups[i][side], start + j) for j in range(SCI)]
            for t in range(side, 2):
                products = [factors[j] * row_far(groups[inner[j // 8]][t], j % 8) for j in range(SCI)]
                groups[i][t] = groups[i][t] - added(products)
        rest = [i for i in range(len(groups)) if i not in inner and i not in ahead]
        left = jnp.concatenate([groups[i][side] for i in rest], axis=0)
        right = jnp.concatenate([jnp.concatenate([groups[i][t] for i in inner], axis=0) for t in range(side, 2)], axis=1)
        padding = [jnp.zeros((n, right.shape[1]), jnp.float32) for n in (start, LANES - start - SLOTS)]
        right = jnp.concatenate([x for x in (padding[0], right, padding[1]) if x.shape[0]], axis=0)
        change = jnp.dot(left, right, precision=lax.Precision.HIGHEST, preferred_element_type=jnp.float32)
        for n, i in enumerate(rest):
            for t in range(side, 2):
                groups[i][t] = groups[i][t] - change[8 * n : 8 * n + 8, (t - side) * LANES : (t - side + 1) * LANES]
    solved = jnp.concatenate([group[1][:, 2 * SLOTS : 2 * SLOTS + 1] for group in groups], axis=0)
    turned = []
    for q in range(NQ):
        part = solved[q * SLOTS : (q + 1) * SLOTS]
        part = jnp.broadcast_to(jnp.concatenate([part] * (LANES // SLOTS), axis=0), (LANES, LANES))
        turned.append(jnp.transpose(part)[0:rows, :])
    row = iota((rows, LANES), 0)
    v = 2.0 * ((strip * rows + row).astype(jnp.float32) + 0.5) / (rows * strip_count) - 1.0
    group = iota((rows, LANES), 1) // SLOTS
    weights = [jnp.zeros((rows, LANES), jnp.float32) for _ in range(3)]
    for q, (a, c) in enumerate(mono_powers):
        weights[a] = weights[a] + turned[q] * (v * v if c == 2 else v if c else jnp.ones_like(v))
    def spread(start, count):
        pieces = []
        for weight in weights:
            tiles = []
            for m in range(-(-count * SLOTS // LANES)):
                place = group + m * (LANES // SLOTS)
                tiles.append(jnp.where((place + start == row) & (place < count), weight, 0.0))
            pieces.append(jnp.concatenate(tiles, axis=1))
        high, low = split_two(jnp.concatenate(pieces, axis=0))
        return jnp.concatenate([high, low], axis=0)[:, : count * SLOTS]

    images = [(spread(*part), ref) for part, ref in zip(row_split(rows), (early_ref, late_ref))]
    u = u_row(cols)
    step = cols // sems.shape[0]
    writes = []
    for n in range(sems.shape[0]):
        at = slice(n * step, (n + 1) * step)
        sums = sum(jnp.dot(x, ref[:, at], preferred_element_type=jnp.float32) for x, ref in images)
        model = [sums[a * rows : (a + 1) * rows] + sums[(a + 3) * rows : (a + 4) * rows] for a in range(3)]
        out_ref[:, at] = science_ref[:, at] - (model[0] + u[:, at] * (model[1] + u[:, at] * model[2]))
        writes.append(pltpu.make_async_copy(out_ref.at[:, at], out_hbm_ref.at[:, at], sems.at[n]))
        writes[n].start()
    for write in writes:
        write.wait()


def body(tile_store, tile_source, tile_slot, shift_cols, spatial_order, science):
    strip_count = lax.axis_size("strip")
    device_count = lax.axis_size("ccd") * strip_count
    rows, cols = science.shape
    vmem = pl.BlockSpec(memory_space=pltpu.VMEM)
    smem = pl.BlockSpec(memory_space=pltpu.SMEM)
    hbm = pl.BlockSpec(memory_space=pltpu.HBM)

    def outside(value):
        return pltpu.with_memory_space_constraint(value, pltpu.HBM)

    def kept(value):
        return pltpu.with_memory_space_constraint(value, pltpu.VMEM)

    tile_store, source, slot, science = map(outside, (tile_store, tile_source.T, tile_slot.T, science))

    def params(mib):
        return pltpu.CompilerParams(vmem_limit_bytes=mib * 1024 * 1024)

    outgoing = pl.pallas_call(
        pack_kernel,
        out_shape=jax.ShapeDtypeStruct((device_count,) + tile_store.shape[1:], jnp.float32),
        in_specs=[hbm, hbm, hbm],
        out_specs=vmem,
        scratch_shapes=[
            pltpu.VMEM(tile_store.shape, jnp.float32),
            pltpu.VMEM(source.shape, jnp.int32),
            pltpu.VMEM(slot.shape, jnp.int32),
            pltpu.SemaphoreType.DMA((3,)),
        ],
        compiler_params=params(60),
        name="pack",
    )(tile_store, source, slot)
    arrived = lax.all_to_all(outgoing, ("ccd", "strip"), split_axis=0, concat_axis=0, tiled=True)
    owner, science, band, *vertical = pl.pallas_call(
        table_kernel,
        out_shape=(
            pltpu.VMEM((tile_source.shape[1], LANES), jnp.int32),
            pltpu.VMEM((rows, cols), jnp.float32),
            pltpu.VMEM((4 * LANES, NF * LANES), jnp.bfloat16),
        )
        + tuple(pltpu.VMEM((rows * HALF, 3 * len(m) * rows), jnp.bfloat16) for m in filter_sets),
        in_specs=[vmem, hbm],
        out_specs=(vmem,) * 5,
        scratch_shapes=[pltpu.SemaphoreType.DMA],
        compiler_params=params(16),
        name="tables",
        cost_estimate=pl.CostEstimate(flops=10_000_000, bytes_accessed=2_000_000, transcendentals=1_000_000),
    )(source, science)
    count = cols // LANES + 1
    edge = -(-count * H // 8) * 8
    window, to_partner, to_other = pl.pallas_call(
        window_kernel,
        out_shape=(
            jax.ShapeDtypeStruct((rows, count * LANES), jnp.float32),
            jax.ShapeDtypeStruct((edge, LANES), jnp.float32),
            jax.ShapeDtypeStruct((edge, LANES), jnp.float32),
        ),
        in_specs=[vmem, vmem, smem],
        out_specs=(vmem, vmem, vmem),
        compiler_params=params(16),
        name="window",
    )(arrived, kept(owner), shift_cols)

    def swap(value, start):
        pairs = [(i, i + 1) for i in range(start, strip_count - 1, 2)]
        return lax.ppermute(value, "strip", pairs + [(j, i) for i, j in pairs])

    from_other = swap(to_other, 1)
    from_partner = swap(to_partner, 0)

    filtered_own = pl.pallas_call(
        own_kernel,
        out_shape=tuple(pltpu.VMEM((len(m) * rows, cols), jnp.bfloat16) for m in filter_sets),
        in_specs=[vmem, vmem],
        out_specs=(vmem, vmem),
        scratch_shapes=[pltpu.VMEM((cols // LANES * rows, NF * LANES), jnp.float32)],
        compiler_params=params(16),
        name="own",
        cost_estimate=pl.CostEstimate(flops=600_000_000, bytes_accessed=3_000_000, transcendentals=0),
    )(window, kept(band))
    packed = -(-len(moment_keys) // 4) * HALF
    halves = tuple(pltpu.VMEM((len(m) * rows, cols), jnp.bfloat16) for m in filter_sets)
    (_, early_count), (_, late_count) = row_split(rows)
    working = [
        pltpu.VMEM((rows, count * LANES), jnp.float32),
        pltpu.VMEM((cols // LANES * rows, NF * LANES), jnp.float32),
    ]
    science = kept(science)
    band, filtered_own, vertical = kept(band), [*map(kept, filtered_own)], [*map(kept, vertical)]
    early, early_moments, *filtered_partner = pl.pallas_call(
        early_kernel,
        out_shape=(
            pltpu.VMEM((early_count * SLOTS, cols), jnp.bfloat16),
            pltpu.VMEM((packed, LANES), jnp.float32),
        )
        + halves,
        in_specs=[vmem] * 7,
        out_specs=(vmem,) * 4,
        scratch_shapes=working,
        compiler_params=params(16),
        name="early",
        cost_estimate=pl.CostEstimate(flops=1_000_000_000, bytes_accessed=4_000_000, transcendentals=0),
    )(*filtered_own, from_partner, science, band, *vertical)
    late, moments = pl.pallas_call(
        late_kernel,
        out_shape=(
            pltpu.VMEM((late_count * SLOTS, cols), jnp.bfloat16),
            pltpu.VMEM((packed, LANES), jnp.float32),
        ),
        in_specs=[vmem] * 10,
        out_specs=(vmem, vmem),
        scratch_shapes=working + [pltpu.VMEM((len(m) * rows, cols), jnp.bfloat16) for m in filter_sets],
        compiler_params=params(24),
        name="late",
    )(*filtered_own, *map(kept, filtered_partner), from_other, kept(early_moments), science, band, *vertical)

    def exchanged(value, step):
        return lax.ppermute(value, "strip", [(i, i ^ step) for i in range(strip_count)])

    moments = moments + exchanged(moments, 1)
    parts = [moments] + [exchanged(moments, step) for step in range(2, strip_count, 2)]

    return pl.pallas_call(
        solve_kernel,
        out_shape=jax.ShapeDtypeStruct((rows, cols), jnp.float32),
        in_specs=[smem, vmem, vmem, vmem] + [vmem] * len(parts),
        out_specs=hbm,
        scratch_shapes=[
            pltpu.VMEM((NQ * SLOTS, 2 * LANES), jnp.float32),
            pltpu.VMEM((rows, cols), jnp.float32),
            pltpu.SemaphoreType.DMA((4,)),
        ],
        compiler_params=params(16),
        name="solve",
    )(spatial_order, science, kept(early), kept(late), *parts)


def solution(mesh):
    placed = (
        P(("ccd", "strip"), None, None),
        P(),
        P(),
        P("ccd"),
        P("ccd"),
        P(("ccd", "strip"), None),
    )
    return jax.shard_map(
        body, mesh=mesh, in_specs=placed, out_specs=P(("ccd", "strip"), None), check_vma=False
    )
```

```python
import functools
import math

import jax
import jax.numpy as jnp
from jax import lax
from jax.experimental import pallas as pl
from jax.experimental.pallas import tpu as pltpu
from jax.sharding import PartitionSpec as P

H = 11
CM = 128
TW = 2304
LANES = 128
SLOTS = 32
TAIL = 32
INSIDE = "promise_in_bounds"

gauss_sigmas = (0.7, 1.5, 3.0)
poly_degrees = (4, 2, 2)
mono_degrees = (0, 1, 1, 2, 2, 2)
mono_powers = ((0, 0), (1, 0), (0, 1), (2, 0), (1, 1), (0, 2))
ridge_weight = 0.05

filters = [(g, n) for g, top in enumerate(poly_degrees) for n in range(top + 1)]
basis_list = [
    (g, i, j) for g, top in enumerate(poly_degrees) for i in range(top + 1) for j in range(top + 1 - i)
]
NF = len(filters)
HALF = SLOTS // 2
filter_sets = [[f for f in filters if f[0] == 0], [f for f in filters if f[0] > 0]]
image_sets = [[b for b in basis_list if b[0] == 0], [b for b in basis_list if b[0] > 0]]
ONE = len(image_sets[0])
SCI = HALF + len(image_sets[1])
moment_keys = [(a, c) for c in range(5) for a in range(5 - c)]
NQ = len(mono_powers)


def envelope_norm(sigma):
    return sum(math.exp(-a * a / (2.0 * sigma * sigma)) for a in range(-H, H + 1))


def iota(shape, dim):
    return lax.broadcasted_iota(jnp.int32, shape, dim)


def split_two(value):
    high = value.astype(jnp.bfloat16)
    low = (value - high.astype(jnp.float32)).astype(jnp.bfloat16)
    return high, low


def pack_kernel(store_hbm_ref, source_hbm_ref, slot_hbm_ref, out_ref, store_ref, source_ref, slot_ref, sems):
    pairs = ((source_hbm_ref, source_ref), (slot_hbm_ref, slot_ref), (store_hbm_ref, store_ref))
    copies = [pltpu.make_async_copy(here, there, sems.at[n]) for n, (here, there) in enumerate(pairs)]
    for copy in copies:
        copy.start()
    me = lax.axis_index("ccd") * lax.axis_size("strip") + lax.axis_index("strip")
    copies[0].wait()
    copies[1].wait()
    source = source_ref[...]
    slots = jnp.sum(jnp.where(source == me, slot_ref[...], 0), axis=0, keepdims=True)
    copies[2].wait()
    for strip in range(out_ref.shape[0]):
        out_ref[strip] = store_ref[slots[0, strip]]


def window_kernel(arrived_ref, owner_ref, shift_ref, window_ref, partner_ref, other_ref):
    even = lax.rem(lax.axis_index("strip"), 2) == 0
    tiles = owner_ref.shape[0]
    rows = arrived_ref.shape[1]
    count = window_ref.shape[1] // LANES
    start = CM - H + shift_ref[0]
    skip = start >= LANES
    offset = start - jnp.where(skip, LANES, 0)
    turn = lax.rem(LANES - offset, LANES)
    stays = iota((rows, LANES), 1) < LANES - offset
    owners = owner_ref[...]
    owners = [owners[t, 0] for t in range(tiles)]
    turned = []
    for w in range(count + 1):
        owner = jnp.where(skip, owners[min(w + 1, tiles - 1)], owners[w])
        turned.append(pltpu.roll(arrived_ref[owner], turn, 1))
    for w in range(count):
        tile = jnp.where(stays, turned[w], turned[w + 1])
        window_ref[:, w * LANES : (w + 1) * LANES] = tile
        last, first = tile[rows - H :], tile[:H]
        partner_ref[w * H : (w + 1) * H, :] = jnp.where(even, last, first)
        other_ref[w * H : (w + 1) * H, :] = jnp.where(even, first, last)
    spare = partner_ref.shape[0] - count * H
    partner_ref[count * H :, :] = jnp.zeros((spare, LANES), jnp.float32)
    other_ref[count * H :, :] = jnp.zeros((spare, LANES), jnp.float32)


def table_kernel(source_ref, science_hbm_ref, owner_ref, science_ref, band_ref, *refs):
    *vertical_refs, sem = refs
    rows = science_ref.shape[0]
    science_copy = pltpu.make_async_copy(science_hbm_ref, science_ref, sem)
    science_copy.start()
    even = lax.rem(lax.axis_index("strip"), 2) == 0
    me = lax.axis_index("ccd") * lax.axis_size("strip") + lax.axis_index("strip")
    source = source_ref[...]
    owner = jnp.sum(jnp.where(iota(source.shape, 1) == me, source, 0), axis=1, keepdims=True)
    owner_ref[...] = jnp.broadcast_to(owner, owner_ref.shape)
    row = iota((LANES, LANES), 0)
    near = row - iota((LANES, LANES), 1) - H
    far = near + LANES - row + row % TAIL
    for f, (g, n) in enumerate(filters):
        sigma = gauss_sigmas[g]
        at = slice(f * LANES, (f + 1) * LANES)
        parts = []
        for place in (near, far):
            offset = place.astype(jnp.float32)
            tap = jnp.exp(-offset * offset / (2.0 * sigma * sigma)) * (1.0 / envelope_norm(sigma))
            for _ in range(n):
                tap = tap * (offset * (1.0 / sigma))
            parts.append(split_two(jnp.where(jnp.abs(place) <= H, tap, 0.0)))
        (near_high, near_low), (far_high, far_low) = parts
        band_ref[0:LANES, at] = near_high
        band_ref[LANES : 2 * LANES, at] = near_high
        band_ref[2 * LANES : 3 * LANES, at] = near_low
        tail = jnp.where(row < 2 * TAIL, far_high.astype(jnp.float32), far_low.astype(jnp.float32))
        band_ref[3 * LANES :, at] = jnp.where(row < 3 * TAIL, tail, 0.0).astype(jnp.bfloat16)
    for vertical_ref, members, images in zip(vertical_refs, filter_sets, image_sets):
        width = vertical_ref.shape[1]
        slot = iota((HALF, width), 0)
        column = iota((HALF, width), 1)
        wanted = jnp.full((HALF, width), -1, jnp.int32)
        degree = jnp.zeros((HALF, width), jnp.int32)
        scale = jnp.ones((HALF, width), jnp.float32)
        weight = jnp.zeros((HALF, width), jnp.float32)
        for b, (g, i, j) in enumerate(images):
            here = slot == b
            wanted = jnp.where(here, members.index((g, i)), wanted)
            degree = jnp.where(here, j, degree)
            scale = jnp.where(here, 1.0 / gauss_sigmas[g], scale)
            weight = jnp.where(here, 1.0 / envelope_norm(gauss_sigmas[g]), weight)
        edge = len(members) * rows
        section = jnp.where(column < edge, 0, jnp.where(column < 2 * edge, 1, 2))
        local = column - section * edge - wanted * rows
        is_own = section == 0
        matched = (local >= 0) & (local < jnp.where(is_own, rows, H)) & (wanted >= 0)
        is_below = (section == 1) == even
        row_in = local + jnp.where(is_own, H, jnp.where(is_below, H + rows, 0))
        for r in range(rows):
            a = row_in - (r + H)
            z = a.astype(jnp.float32) * scale
            tap = jnp.exp(-0.5 * z * z) * weight
            square = z * z
            power = jnp.where(degree == 1, z, jnp.where(degree == 2, square, 1.0))
            power = jnp.where(degree == 3, square * z, jnp.where(degree == 4, square * square, power))
            keep = matched & (jnp.abs(a) <= H)
            vertical_ref[r * HALF : (r + 1) * HALF, :] = jnp.where(keep, tap * power, 0.0).astype(jnp.bfloat16)
    science_copy.wait()


def wide_tile(value):
    return jnp.concatenate([value, jnp.zeros((value.shape[0], LANES - value.shape[1]), value.dtype)], axis=1)


def turn_lanes(value, by):
    if value.shape[1] < LANES:
        value = wide_tile(value)
    return pltpu.roll(value, by % LANES, 1) if by % LANES else value


def u_row(cols):
    return 2.0 * (iota((1, cols), 1).astype(jnp.float32) + 0.5) / cols - 1.0


def filter_rows(padded, band_ref, filtered_ref, out_refs):
    count = padded.shape[0]
    blocks = filtered_ref.shape[0] // count
    lane = iota((count, LANES), 1)
    window, tails = [], []
    for w in range(blocks + 1):
        tile = padded[:, w * LANES : (w + 1) * LANES]
        high, low = split_two(tile)
        window.append((high, low))
        high, low = high.astype(jnp.float32), low.astype(jnp.float32)
        tail = jnp.where(lane < 2 * TAIL, pltpu.roll(low, TAIL, 1), pltpu.roll(high, 2 * TAIL, 1))
        tails.append(jnp.where(lane < TAIL, high, tail).astype(jnp.bfloat16))
    left = []
    for w in range(blocks):
        high, low = window[w]
        left.append(jnp.concatenate([high, low, high, tails[w + 1]], axis=1))
    filtered_ref[...] = jnp.dot(
        jnp.concatenate(left, axis=0), band_ref[...], preferred_element_type=jnp.float32
    )
    for w in range(blocks):
        for out_ref, members in zip(out_refs, filter_sets):
            first = filters.index(members[0])
            out_ref[:, w * LANES : (w + 1) * LANES] = jnp.concatenate(
                [
                    filtered_ref[w * count : (w + 1) * count, f * LANES : (f + 1) * LANES]
                    for f in range(first, first + len(members))
                ],
                axis=0,
            ).astype(jnp.bfloat16)


def own_kernel(window_ref, band_ref, *refs):
    filter_rows(window_ref[...], band_ref, refs[-1], refs[:-1])


def row_split(rows):
    even = lax.rem(lax.axis_index("strip"), 2) == 0
    return (jnp.where(even, H, 0), rows - H), (jnp.where(even, 0, rows - H), H)


def filter_halo(halo_ref, band_ref, padded_ref, filtered_ref, out_refs):
    rows = padded_ref.shape[0]
    padded_ref[H:, :] = jnp.zeros((rows - H, padded_ref.shape[1]), jnp.float32)
    for w in range(padded_ref.shape[1] // LANES):
        padded_ref[0:H, w * LANES : (w + 1) * LANES] = halo_ref[w * H : (w + 1) * H, :]
    filter_rows(padded_ref[...], band_ref, filtered_ref, out_refs)


def images_and_moments(start, count, vertical_refs, source_refs, science_ref, basis_ref):
    strip_count = lax.axis_size("strip")
    strip = lax.axis_index("strip")
    rows, cols = science_ref.shape
    eighth = iota((8, 2 * LANES), 0)
    for pair in range(cols // LANES // 2):
        at = slice(pair * 2 * LANES, (pair + 1) * 2 * LANES)
        blocks = []
        for n, vertical_ref in enumerate(vertical_refs):
            right = jnp.concatenate([refs[n][:, at] for refs in source_refs], axis=0)
            left = vertical_ref[pl.ds(pl.multiple_of(start * HALF, HALF), count * HALF), 0 : right.shape[0]]
            blocks.append(jnp.dot(left, right, preferred_element_type=jnp.float32))
        one, two = blocks
        parts = []
        for r in range(count):
            low, high = r * HALF, (r + 1) * HALF
            science = science_ref[pl.ds(start + r, 1), at]
            parts += [one[low : high - 8], jnp.where(eighth == ONE % 8, 1.0, one[high - 8 : high])]
            parts += [two[low : high - 8], jnp.where(eighth == SCI % 8, science, two[high - 8 : high])]
        basis_ref[:, at] = jnp.concatenate(parts, axis=0).astype(jnp.bfloat16)

    u = u_row(cols)
    square = u * u
    totals = [None] * 5
    for r in range(count):
        here = basis_ref[r * SLOTS : (r + 1) * SLOTS, :]
        wide = here.astype(jnp.float32)
        once, twice = (wide * u).astype(jnp.bfloat16), (wide * square).astype(jnp.bfloat16)
        product = lax.dot_general(
            jnp.concatenate([here, once, twice], axis=0),
            jnp.concatenate([here, twice], axis=0),
            (((1,), (1,)), ((), ())),
            preferred_element_type=jnp.float32,
        )
        v = 2.0 * ((strip * rows + start + r).astype(jnp.float32) + 0.5) / (rows * strip_count) - 1.0
        for c in range(5):
            totals[c] = product if totals[c] is None else totals[c] + product
            product = product * v
    row = iota((HALF, LANES), 0)
    lane = iota((HALF, LANES), 1)
    chunks = [jnp.zeros((HALF, LANES), jnp.float32) for _ in range(-(-len(moment_keys) // 4))]
    for at, (a, c) in enumerate(moment_keys):
        first, second = (a, 0) if a < 3 else (a - 2, 1)
        group = at % 4 * SLOTS
        top = totals[c][first * SLOTS : first * SLOTS + HALF, :]
        bottom = totals[c][first * SLOTS + HALF : (first + 1) * SLOTS, :]
        by = group - second * SLOTS
        corner = jnp.where(lane - group - HALF <= row, turn_lanes(top, by + HALF), turn_lanes(bottom, by + 1))
        both = jnp.where(lane - group < HALF, turn_lanes(bottom, by), corner)
        chunks[at // 4] = jnp.where(lane // SLOTS == at % 4, both, chunks[at // 4])
    return jnp.concatenate(chunks, axis=0)


def early_kernel(
    first_own_ref, second_own_ref, partner_ref, science_ref, band_ref, first_ref, second_ref,
    basis_ref, moment_ref, first_partner_ref, second_partner_ref,
    padded_ref, filtered_ref,
):
    partner_refs = first_partner_ref, second_partner_ref
    filter_halo(partner_ref, band_ref, padded_ref, filtered_ref, partner_refs)
    start, count = row_split(science_ref.shape[0])[0]
    sources = (first_own_ref, second_own_ref), partner_refs
    moment_ref[...] = images_and_moments(start, count, (first_ref, second_ref), sources, science_ref, basis_ref)


def late_kernel(
    first_own_ref, second_own_ref, first_partner_ref, second_partner_ref, other_ref, early_ref,
    science_ref, band_ref, first_ref, second_ref,
    basis_ref, moment_ref,
    padded_ref, filtered_ref, first_other_ref, second_other_ref,
):
    other_refs = first_other_ref, second_other_ref
    filter_halo(other_ref, band_ref, padded_ref, filtered_ref, other_refs)
    start, count = row_split(science_ref.shape[0])[1]
    sources = (first_own_ref, second_own_ref), (first_partner_ref, second_partner_ref), other_refs
    moments = images_and_moments(start, count, (first_ref, second_ref), sources, science_ref, basis_ref)
    moment_ref[...] = early_ref[...] + moments


def solve_kernel(order_ref, science_ref, early_ref, late_ref, *refs):
    out_hbm_ref, system_ref, out_ref, sems = refs[-4:]
    strip_count = lax.axis_size("strip")
    strip = lax.axis_index("strip")
    rows, cols = science_ref.shape
    order = order_ref[0]
    total = refs[0][...]
    for ref in refs[1:-4]:
        total = total + ref[...]
    half = SLOTS // 2
    across = jnp.transpose(jnp.concatenate([total, jnp.zeros((LANES - total.shape[0], LANES), jnp.float32)], axis=0))
    next_across = pltpu.roll(across, LANES - 1, 0)
    half_row = iota((half, LANES), 0)
    half_lane = iota((half, LANES), 1)
    pieces = {}
    for at, key in enumerate(moment_keys):
        here = total[at // 4 * half : (at // 4 + 1) * half, :]
        group, place = at % 4 * SLOTS, at // 4 * half
        first = across[group : group + half, :]
        second = across[group + half : group + SLOTS, :]
        shifted = next_across[group + half : group + SLOTS, :]
        corner = jnp.where(
            half_lane <= half_row, turn_lanes(here, -group - half), turn_lanes(second, -place)
        )
        top = jnp.where(half_lane < half, corner, turn_lanes(first, half - place))
        corner = jnp.where(
            half_lane - half >= half_row, turn_lanes(here, -group - 1), turn_lanes(shifted, half - place)
        )
        bottom = jnp.where(half_lane < half, turn_lanes(here, -group), corner)
        pieces[key] = jnp.concatenate([top, bottom], axis=0)
    lane = iota((SLOTS, LANES), 1)
    lane_slot = lane & (SLOTS - 1)
    lane_group = lane // SLOTS
    row_slot = iota((SLOTS, LANES), 0)

    def active(slot, q):
        return ((slot < SCI) & (slot != ONE) & (mono_degrees[q] <= order)) | (slot == ONE)

    def moved(key, to_lane, from_lane):
        return turn_lanes(pieces[key], to_lane - from_lane)

    for q, (aq, cq) in enumerate(mono_powers):
        tiles = [jnp.zeros((SLOTS, LANES), jnp.float32) for _ in range(2)]
        for k, (ak, ck) in enumerate(mono_powers):
            keep = (lane_group == k % 4) & active(lane_slot, k)
            tiles[k // 4] = jnp.where(keep, moved((aq + ak, cq + ck), (k % 4) * SLOTS, 0), tiles[k // 4])
        tiles[1] = jnp.where(lane == 2 * SLOTS, moved((aq, cq), 2 * SLOTS, SCI), tiles[1])
        row_on = active(row_slot, q)
        for side in range(2):
            tile = jnp.where(row_on, tiles[side], 0.0)
            if q // 4 == side:
                diagonal = lane == row_slot + (q % 4) * SLOTS
                weight = jnp.where(row_on, tile, 1.0) * (1.0 + ridge_weight)
                tile = jnp.where(diagonal, weight, tile)
            system_ref[q * SLOTS : (q + 1) * SLOTS, side * LANES : (side + 1) * LANES] = tile

    row8 = iota((8, LANES), 0)

    def column(value, at):
        return jnp.take_along_axis(value, jnp.full((8, LANES), at, jnp.int32), axis=1, mode=INSIDE)

    def added(terms):
        while len(terms) > 1:
            terms = [sum(terms[n + 1 : n + 2], terms[n]) for n in range(0, len(terms), 2)]
        return terms[0]

    def column_far(value, at):
        return jnp.broadcast_to(value[:, at : at + 1], (8, LANES))

    def row_far(value, at):
        return jnp.broadcast_to(value[at : at + 1, :], (8, LANES))

    def row_of(value, at):
        return jnp.take_along_axis(value, jnp.full((8, LANES), at, jnp.int32), axis=0, mode=INSIDE)

    per = SLOTS // 8

    def eliminate(top):
        groups = [
            [system_ref[8 * i : 8 * i + 8, side * LANES : (side + 1) * LANES] for side in range(2)]
            for i in range(NQ * SLOTS // 8)
        ]
        for q in range(NQ):
            side, start = divmod(q * SLOTS, LANES)
            if mono_degrees[q] > top:
                place = q * per + ONE // 8
                pivot = groups[place][side][ONE % 8 : ONE % 8 + 1, start + ONE : start + ONE + 1]
                inverse = 1.0 / jnp.broadcast_to(pivot, (8, LANES))
                ready = [row_of(tile, ONE % 8) * inverse for tile in groups[place][side:]]
                for i in range(len(groups)):
                    factor = column(groups[i][side], start + ONE)
                    for t in range(side, 2):
                        changed = groups[i][t] - factor * ready[t - side]
                        if i == place:
                            changed = jnp.where(row8 == ONE % 8, ready[t - side], changed)
                        groups[i][t] = changed
                continue
            inner = list(range(q * per, (q + 1) * per))
            for block in inner:
                first = 8 * block % LANES
                count = min(8, SCI - 8 * block % SLOTS)
                panel = [column(groups[block][side], first + j) for j in range(count)] + groups[block][side:]
                known = None
                for k in range(0, count, 2):
                    one, two = panel[k], panel[k + 1]
                    if known is None:
                        known = [row_of(x, i) for i in (k, k + 1) for x in (one, two)]
                    a, b, c, d = known
                    inverse = 1.0 / (a * d - b * c)
                    pairs = [(row_of(x, k), row_of(x, k + 1)) for x in panel]
                    first_rest, second_rest = two * c - one * d, one * b - two * a
                    if k + 2 < count:
                        known = []
                        for i in (k + 2, k + 3):
                            before, after = row_of(one, i), row_of(two, i)
                            first_here, second_here = after * c - before * d, before * b - after * a
                            for j in (k + 2, k + 3):
                                step = first_here * pairs[j][0] + second_here * pairs[j][1]
                                known.append(row_of(panel[j], i) + inverse * step)
                    here, after = row8 == k, row8 == k + 1
                    first_factor = inverse * jnp.where(here, d, jnp.where(after, -c, first_rest))
                    second_factor = inverse * jnp.where(here, -b, jnp.where(after, a, second_rest))
                    for j in range(k + 2, len(panel)):
                        old = jnp.where(here | after, 0.0, panel[j])
                        panel[j] = old + (first_factor * pairs[j][0] + second_factor * pairs[j][1])
                ready = panel[count:]
                spread_rows = [[row_far(tile, j) for j in range(count)] for tile in ready]
                groups[block][side:] = ready
                for i in inner:
                    if i != block:
                        factors = [column_far(groups[i][side], first + j) for j in range(count)]
                        for t in range(side, 2):
                            products = [factors[j] * spread_rows[t - side][j] for j in range(count)]
                            groups[i][t] = groups[i][t] - added(products)
            ahead = list(range((q + 1) * per, (q + 2) * per)) if q + 1 < NQ else []
            for i in ahead:
                factors = [column_far(groups[i][side], start + j) for j in range(SCI)]
                for t in range(side, 2):
                    products = [factors[j] * row_far(groups[inner[j // 8]][t], j % 8) for j in range(SCI)]
                    groups[i][t] = groups[i][t] - added(products)
            rest = [i for i in range(len(groups)) if i not in inner and i not in ahead]
            left = jnp.concatenate([groups[i][side] for i in rest], axis=0)
            right = jnp.concatenate([jnp.concatenate([groups[i][t] for i in inner], axis=0) for t in range(side, 2)], axis=1)
            padding = [jnp.zeros((n, right.shape[1]), jnp.float32) for n in (start, LANES - start - SLOTS)]
            right = jnp.concatenate([x for x in (padding[0], right, padding[1]) if x.shape[0]], axis=0)
            change = jnp.dot(left, right, precision=lax.Precision.HIGHEST, preferred_element_type=jnp.float32)
            for n, i in enumerate(rest):
                for t in range(side, 2):
                    groups[i][t] = groups[i][t] - change[8 * n : 8 * n + 8, (t - side) * LANES : (t - side + 1) * LANES]
        for i, group in enumerate(groups):
            system_ref[8 * i : 8 * i + 8, LANES:] = group[1]

    for top in range(max(mono_degrees) + 1):
        pl.when(order == top)(functools.partial(eliminate, top))
    solved = system_ref[:, LANES + 2 * SLOTS : LANES + 2 * SLOTS + 1]
    turned = []
    for q in range(NQ):
        part = solved[q * SLOTS : (q + 1) * SLOTS]
        part = jnp.broadcast_to(jnp.concatenate([part] * (LANES // SLOTS), axis=0), (LANES, LANES))
        turned.append(jnp.transpose(part)[0:rows, :])
    row = iota((rows, LANES), 0)
    v = 2.0 * ((strip * rows + row).astype(jnp.float32) + 0.5) / (rows * strip_count) - 1.0
    group = iota((rows, LANES), 1) // SLOTS
    weights = [jnp.zeros((rows, LANES), jnp.float32) for _ in range(3)]
    for q, (a, c) in enumerate(mono_powers):
        weights[a] = weights[a] + turned[q] * (v * v if c == 2 else v if c else jnp.ones_like(v))
    def spread(start, count):
        pieces = []
        for weight in weights:
            tiles = []
            for m in range(-(-count * SLOTS // LANES)):
                place = group + m * (LANES // SLOTS)
                tiles.append(jnp.where((place + start == row) & (place < count), weight, 0.0))
            pieces.append(jnp.concatenate(tiles, axis=1))
        high, low = split_two(jnp.concatenate(pieces, axis=0))
        return jnp.concatenate([high, low], axis=0)[:, : count * SLOTS]

    images = [(spread(*part), ref) for part, ref in zip(row_split(rows), (early_ref, late_ref))]
    u = u_row(cols)
    step = cols // sems.shape[0]
    writes = []
    for n in range(sems.shape[0]):
        at = slice(n * step, (n + 1) * step)
        sums = sum(jnp.dot(x, ref[:, at], preferred_element_type=jnp.float32) for x, ref in images)
        model = [sums[a * rows : (a + 1) * rows] + sums[(a + 3) * rows : (a + 4) * rows] for a in range(3)]
        out_ref[:, at] = science_ref[:, at] - (model[0] + u[:, at] * (model[1] + u[:, at] * model[2]))
        writes.append(pltpu.make_async_copy(out_ref.at[:, at], out_hbm_ref.at[:, at], sems.at[n]))
        writes[n].start()
    for write in writes:
        write.wait()


def body(tile_store, tile_source, tile_slot, shift_cols, spatial_order, science):
    strip_count = lax.axis_size("strip")
    device_count = lax.axis_size("ccd") * strip_count
    rows, cols = science.shape
    vmem = pl.BlockSpec(memory_space=pltpu.VMEM)
    smem = pl.BlockSpec(memory_space=pltpu.SMEM)
    hbm = pl.BlockSpec(memory_space=pltpu.HBM)

    def outside(value):
        return pltpu.with_memory_space_constraint(value, pltpu.HBM)

    def kept(value):
        return pltpu.with_memory_space_constraint(value, pltpu.VMEM)

    tile_store, source, slot, science = map(outside, (tile_store, tile_source.T, tile_slot.T, science))

    def params(mib):
        return pltpu.CompilerParams(vmem_limit_bytes=mib * 1024 * 1024)

    outgoing = pl.pallas_call(
        pack_kernel,
        out_shape=jax.ShapeDtypeStruct((device_count,) + tile_store.shape[1:], jnp.float32),
        in_specs=[hbm, hbm, hbm],
        out_specs=vmem,
        scratch_shapes=[
            pltpu.VMEM(tile_store.shape, jnp.float32),
            pltpu.VMEM(source.shape, jnp.int32),
            pltpu.VMEM(slot.shape, jnp.int32),
            pltpu.SemaphoreType.DMA((3,)),
        ],
        compiler_params=params(60),
        name="pack",
    )(tile_store, source, slot)
    arrived = lax.all_to_all(outgoing, ("ccd", "strip"), split_axis=0, concat_axis=0, tiled=True)
    owner, science, band, *vertical = pl.pallas_call(
        table_kernel,
        out_shape=(
            pltpu.VMEM((tile_source.shape[1], LANES), jnp.int32),
            pltpu.VMEM((rows, cols), jnp.float32),
            pltpu.VMEM((4 * LANES, NF * LANES), jnp.bfloat16),
        )
        + tuple(pltpu.VMEM((rows * HALF, 3 * len(m) * rows), jnp.bfloat16) for m in filter_sets),
        in_specs=[vmem, hbm],
        out_specs=(vmem,) * 5,
        scratch_shapes=[pltpu.SemaphoreType.DMA],
        compiler_params=params(16),
        name="tables",
        cost_estimate=pl.CostEstimate(flops=10_000_000, bytes_accessed=2_000_000, transcendentals=1_000_000),
    )(source, science)
    count = cols // LANES + 1
    edge = -(-count * H // 8) * 8
    window, to_partner, to_other = pl.pallas_call(
        window_kernel,
        out_shape=(
            jax.ShapeDtypeStruct((rows, count * LANES), jnp.float32),
            jax.ShapeDtypeStruct((edge, LANES), jnp.float32),
            jax.ShapeDtypeStruct((edge, LANES), jnp.float32),
        ),
        in_specs=[vmem, vmem, smem],
        out_specs=(vmem, vmem, vmem),
        compiler_params=params(16),
        name="window",
    )(arrived, kept(owner), shift_cols)

    def swap(value, start):
        pairs = [(i, i + 1) for i in range(start, strip_count - 1, 2)]
        return lax.ppermute(value, "strip", pairs + [(j, i) for i, j in pairs])

    from_other = swap(to_other, 1)
    from_partner = swap(to_partner, 0)

    filtered_own = pl.pallas_call(
        own_kernel,
        out_shape=tuple(pltpu.VMEM((len(m) * rows, cols), jnp.bfloat16) for m in filter_sets),
        in_specs=[vmem, vmem],
        out_specs=(vmem, vmem),
        scratch_shapes=[pltpu.VMEM((cols // LANES * rows, NF * LANES), jnp.float32)],
        compiler_params=params(16),
        name="own",
        cost_estimate=pl.CostEstimate(flops=600_000_000, bytes_accessed=3_000_000, transcendentals=0),
    )(window, kept(band))
    packed = -(-len(moment_keys) // 4) * HALF
    halves = tuple(pltpu.VMEM((len(m) * rows, cols), jnp.bfloat16) for m in filter_sets)
    (_, early_count), (_, late_count) = row_split(rows)
    working = [
        pltpu.VMEM((rows, count * LANES), jnp.float32),
        pltpu.VMEM((cols // LANES * rows, NF * LANES), jnp.float32),
    ]
    science = kept(science)
    band, filtered_own, vertical = kept(band), [*map(kept, filtered_own)], [*map(kept, vertical)]
    early, early_moments, *filtered_partner = pl.pallas_call(
        early_kernel,
        out_shape=(
            pltpu.VMEM((early_count * SLOTS, cols), jnp.bfloat16),
            pltpu.VMEM((packed, LANES), jnp.float32),
        )
        + halves,
        in_specs=[vmem] * 7,
        out_specs=(vmem,) * 4,
        scratch_shapes=working,
        compiler_params=params(16),
        name="early",
        cost_estimate=pl.CostEstimate(flops=1_000_000_000, bytes_accessed=4_000_000, transcendentals=0),
    )(*filtered_own, from_partner, science, band, *vertical)
    late, moments = pl.pallas_call(
        late_kernel,
        out_shape=(
            pltpu.VMEM((late_count * SLOTS, cols), jnp.bfloat16),
            pltpu.VMEM((packed, LANES), jnp.float32),
        ),
        in_specs=[vmem] * 10,
        out_specs=(vmem, vmem),
        scratch_shapes=working + [pltpu.VMEM((len(m) * rows, cols), jnp.bfloat16) for m in filter_sets],
        compiler_params=params(24),
        name="late",
    )(*filtered_own, *map(kept, filtered_partner), from_other, kept(early_moments), science, band, *vertical)

    def exchanged(value, step):
        return lax.ppermute(value, "strip", [(i, i ^ step) for i in range(strip_count)])

    moments = moments + exchanged(moments, 1)
    parts = [moments] + [exchanged(moments, step) for step in range(2, strip_count, 2)]

    return pl.pallas_call(
        solve_kernel,
        out_shape=jax.ShapeDtypeStruct((rows, cols), jnp.float32),
        in_specs=[smem, vmem, vmem, vmem] + [vmem] * len(parts),
        out_specs=hbm,
        scratch_shapes=[
            pltpu.VMEM((NQ * SLOTS, 2 * LANES), jnp.float32),
            pltpu.VMEM((rows, cols), jnp.float32),
            pltpu.SemaphoreType.DMA((4,)),
        ],
        compiler_params=params(16),
        name="solve",
    )(spatial_order, science, kept(early), kept(late), *parts)


def solution(mesh):
    placed = (
        P(("ccd", "strip"), None, None),
        P(),
        P(),
        P("ccd"),
        P("ccd"),
        P(("ccd", "strip"), None),
    )
    return jax.shard_map(
        body, mesh=mesh, in_specs=placed, out_specs=P(("ccd", "strip"), None), check_vma=False
    )
```
